32 devices in a mesh: slab: 2 (over y), grid: 4 (over z), stack: 4 (over x, core).
Axes of the slice: x: 2, y: 2, z: 4, core: 2. Of those that a mesh axis runs over, the one named last changes fastest.
Arguments:
- disp: float32 [8, 2, 32, 4096], P(('slab', 'stack'), None, 'grid'), parts along dimension 0, may hold values from -6 to 6
- targets: float32 [8, 2, 32, 4096], P(('slab', 'stack'), None, 'grid'), parts along dimension 0, may hold values from -6 to 6
- stiffness: float32 [8], replicated, may hold values from 0.03 to 0.15
- stiff_class: int32 [8, 32, 32], P(('slab', 'stack'), 'grid'), parts along dimension 0, may hold values from 0 to 7
- match_dest: int32 [8, 32, 32], P(('slab', 'stack'), 'grid'), parts along dimension 0, may hold values from -1 to 1023, as said below
Outputs:
- moved: float32 [8, 2, 32, 4096], P(('slab', 'stack'), None, 'grid'), parts along dimension 0
- velocity: float32 [8, 2, 32, 4096], P(('slab', 'stack'), None, 'grid'), parts along dimension 0
The draws below stay inside these ranges and needn't reach their ends.
There are 2 independent parts, one for each index of `slab`. The reference program is written for one: setup_inputs(seed, part) draws one part's arguments, and reference() takes and returns one part's arrays. A program takes and returns all parts, laid end to end along the dimension named above; an argument that names none is the same for every part. Nothing has to cross between parts.
Inputs may be any that keep to these rules, and one draw needn't show every extreme that they name: `match_dest`: each entry is -1 or a block number of the next section; every entry of the last section is -1. From the rows of one grid index, at most 128 blocks are matched into the rows of any one grid index, and in every section but the last some grid index receives exactly 128 from every grid index.
All inputs are finite; a program needn't handle non-finite values.
Results may differ from the reference program's by a relative error of at most 0.00027.
Values sent between devices are 32-bit elements; how exact they have to be, the bound alone decides.
A program may use at most 64 MiB of HBM per device.

```python
import math
import jax
import jax.numpy as jnp

COLS = 4096
ROWS_DEV = 8
BLOCK = 128
CLASSES = 8
STEPS = 8
SECTIONS = 4
ROWS = 32
BLOCKS_ROW = 32
CAP = 128
N_GRID = 4


def draw_match_dest(key, part):
    key = jax.random.fold_in(key, 7)
    subkeys = jax.random.split(key, 6)
    per_band = ROWS_DEV * BLOCKS_ROW
    extent = (SECTIONS, N_GRID, per_band)
    first_pick = jax.random.randint(subkeys[0], extent, 0, N_GRID)
    second_pick = jax.random.randint(subkeys[1], extent, 0, N_GRID)
    band_of = jnp.maximum(first_pick, second_pick)
    hot_band = jax.random.randint(subkeys[2], (SECTIONS, 1, 1), 0, N_GRID - 1)
    position = jnp.arange(per_band)[None, None, :]
    band_of = jnp.where(position < CAP, hot_band, band_of)
    band_of = jnp.where(position == CAP, N_GRID - 1, band_of)
    chosen = jax.random.randint(subkeys[3], extent, 0, 4) != 0
    chosen = chosen | (position <= CAP)
    member = ((band_of[..., None] == jnp.arange(N_GRID)) & chosen[..., None]).astype(jnp.int32)
    ranking = jnp.sum(jnp.cumsum(member, axis=2) * member, axis=3) - 1
    alive = chosen & (ranking < CAP)
    row_pick = jax.random.randint(subkeys[4], extent, 0, ROWS_DEV)
    col_pick = jax.random.randint(subkeys[5], extent, 0, BLOCKS_ROW)
    row_pick = jnp.where(position == CAP, ROWS_DEV - 1, row_pick)
    col_pick = jnp.where(position == CAP, BLOCKS_ROW - 1, col_pick)
    target_block = (band_of * ROWS_DEV + row_pick) * BLOCKS_ROW + col_pick
    section_ok = (jnp.arange(SECTIONS) < SECTIONS - 1)[:, None, None]
    result = jnp.where(alive & section_ok, target_block, -1)
    return result.reshape(SECTIONS, N_GRID * ROWS_DEV, BLOCKS_ROW).astype(jnp.int32)


def touch_ends(values, rng, least, high):
    longest = values.shape.index(max(values.shape))
    spots = []
    for shift in (0, 1):
        where = [jax.random.randint(jax.random.fold_in(rng, axis), (), 0, length) for axis, length in enumerate(values.shape)]
        where[longest] = (where[longest] + shift) % values.shape[longest]
        spots.append(tuple(where))
    return values.at[spots[0]].set(least).at[spots[1]].set(high)


def shard_levels(rng, shape, pieces, least, top_value):
    factor_of = 1.0
    for dim, blocks in pieces:
        steps = jax.random.uniform(jax.random.fold_in(jax.random.fold_in(rng, 6), dim), (blocks,), jnp.float32, least / len(pieces), top_value / len(pieces))
        factor_of = factor_of * jnp.repeat(jnp.exp(steps), shape[dim] // blocks).reshape((-1,) + (1,) * (len(shape) - 1 - dim))
    return factor_of


def scatter_about(own_key, shape, width, most, shards=(), dtype=jnp.bfloat16):
    level = shard_levels(own_key, shape, shards, -0.22, 0.18) if shards else 1.0
    entries = jax.random.normal(own_key, shape, jnp.float32) * width * level
    return jnp.minimum(jnp.maximum(entries, -most), most).astype(dtype)


def setup_inputs(seed: int = 0, part: int = 0) -> dict:
    streams_of = jax.random.split(jax.random.key(seed), 6)
    part_splits = jax.random.split(jax.random.fold_in(streams_of[5], part), 6)
    disp = scatter_about(part_splits[0], (SECTIONS, 2, ROWS, COLS), 1.0, 6.0, ((0, 4), (2, 4)), jnp.float32)
    targets = scatter_about(part_splits[1], (SECTIONS, 2, ROWS, COLS), 1.0, 6.0, ((0, 4), (2, 4)), jnp.float32)
    stiffness = jnp.clip(jnp.exp(jax.random.uniform(streams_of[2], (CLASSES,), jnp.float32, math.log(0.03), math.log(0.15))), 0.03, 0.15)
    stiff_class = touch_ends(jax.random.randint(part_splits[3], (SECTIONS, ROWS, BLOCKS_ROW), 0, CLASSES), jax.random.fold_in(part_splits[3], 1), 0, CLASSES - 1).astype(jnp.int32)
    match_dest = draw_match_dest(jax.random.fold_in(jax.random.fold_in(streams_of[5], part), 71), part)
    return {"disp": disp, "targets": targets, "stiffness": stiffness, "stiff_class": stiff_class, "match_dest": match_dest}


match_gain = 0.1
damping = 0.5


def laplace(field):
    padded = jnp.pad(field, ((0, 0), (0, 0), (1, 1), (1, 1)))
    centre = padded[:, :, 1:-1, 1:-1]
    edge_sum = padded[:, :, 2:, 1:-1] + padded[:, :, :-2, 1:-1] + padded[:, :, 1:-1, 2:] + padded[:, :, 1:-1, :-2]
    corner_sum = padded[:, :, 2:, 2:] + padded[:, :, 2:, :-2] + padded[:, :, :-2, 2:] + padded[:, :, :-2, :-2]
    return edge_sum + 0.5 * corner_sum - 6.0 * centre


def reference(disp, targets, stiffness, stiff_class, match_dest):
    block_total = ROWS * BLOCKS_ROW
    member = (stiff_class[..., None] == jnp.arange(CLASSES).astype(jnp.int32)).astype(jnp.float32)
    kappa_block = jnp.sum(member * stiffness, axis=-1)
    kappa = jnp.repeat(kappa_block, BLOCK, axis=-1)[:, None]
    chosen = match_dest.reshape(SECTIONS, block_total)[: SECTIONS - 1]
    alive = (chosen >= 0).astype(jnp.float32)[:, None, :, None]
    clipped = jnp.maximum(chosen, 0).astype(jnp.int32)
    field = disp
    velocity = jnp.zeros_like(disp)
    for repeat_index in range(STEPS):
        blocks = field.reshape(SECTIONS, 2, block_total, BLOCK)
        pulled = (field - targets).reshape(SECTIONS, 2, block_total, BLOCK)
        ahead = jax.vmap(lambda source, picks: source[:, picks])(blocks[1:], clipped)
        paired = match_gain * alive * (ahead - pulled[:-1])
        reaction = jax.vmap(
            lambda picks, values: jnp.zeros((2, block_total, BLOCK), jnp.float32).at[:, picks].add(values)
        )(clipped, paired)
        match_force = jnp.zeros_like(blocks).at[: SECTIONS - 1].add(paired).at[1:].add(-reaction)
        velocity = damping * velocity + kappa * laplace(field) + match_force.reshape(field.shape)
        field = field + velocity
    return field, velocity
```

```python
import functools

import jax
import jax.numpy as jnp
from jax import lax
from jax.experimental import pallas as pl
from jax.experimental.pallas import tpu as pltpu
from jax.sharding import Mesh
from jax.sharding import PartitionSpec as P

BLOCK = 128
CLASSES = 8
STEPS = 8


match_gain = 0.1
damping = 0.5


def with_halo(value, sides, width):
    for axis, dim in sides:
        peers, length = (lax.axis_size(axis), value.shape[dim])
        up = [(i, (i + 1) % peers) for i in range(peers - 1)]
        down = [(j, i) for i, j in up]
        last = lax.slice_in_dim(value, length - width, length, axis=dim)
        first = lax.slice_in_dim(value, 0, width, axis=dim)
        before = lax.ppermute(last, axis, up)
        after = lax.ppermute(first, axis, down)
        value = jnp.concatenate([before, value, after], axis=dim)
    return value


def passed_along(value, axis, steps):
    count = lax.axis_size(axis)
    first, last = (max(0, -steps), min(count, count - steps))
    return lax.ppermute(value, axis, [(source, source + steps) for source in range(first, last)])


def laplace(extended):
    padded = jnp.pad(extended, ((0, 0), (0, 0), (1, 1)))
    centre = padded[:, 1:-1, 1:-1]
    edge_sum = (
        padded[:, 2:, 1:-1] + padded[:, :-2, 1:-1] + padded[:, 1:-1, 2:] + padded[:, 1:-1, :-2]
    )
    corner_sum = padded[:, 2:, 2:] + padded[:, 2:, :-2] + padded[:, :-2, 2:] + padded[:, :-2, :-2]
    return edge_sum + 0.5 * corner_sum - 6.0 * centre


def placement(marker, block_count, band_count, capacity):
    alive = marker > 0
    target_block = jnp.maximum(marker - 1, 0)
    band_of = target_block // block_count
    member = ((band_of[:, None] == jnp.arange(band_count)[None, :]) & alive[:, None]).astype(
        jnp.int32
    )
    ranking = jnp.sum(jnp.cumsum(member, axis=0) * member, axis=1) - 1
    slot_of = jnp.where(alive, band_of * capacity + ranking, band_count * capacity)
    local_plus = jnp.where(alive, target_block % block_count + 1, 0)
    slot_total = band_count * capacity
    matching = slot_of[None, :] == jnp.arange(slot_total)[:, None]
    route_matrix = matching.astype(jnp.float32)
    labels = jnp.sum(jnp.where(matching, local_plus[None, :], 0), axis=1)
    return (route_matrix, labels)


def gather_slots(route_matrix, values):
    return jnp.einsum("sb,cbk->csk", route_matrix, values, precision=lax.Precision.HIGHEST)


def spread_slots(route_matrix, values):
    return jnp.einsum("sb,csk->cbk", route_matrix, values, precision=lax.Precision.HIGHEST)


def pack(values, route_matrix, labels, band_count, capacity):
    payload = gather_slots(route_matrix, values)
    return (
        payload.reshape(2, band_count, capacity, BLOCK),
        labels.reshape(1, band_count, capacity),
    )


def settle(blocks, payload, labels):
    block_count = blocks.shape[1]
    flat_payload = payload.reshape(2, -1, BLOCK)
    flat_labels = labels.reshape(-1)
    slot_selector = (flat_labels[:, None] - 1 == jnp.arange(block_count)[None, :]).astype(
        jnp.float32
    )
    alive = (flat_labels > 0).astype(jnp.float32)[None, :, None]
    picked = gather_slots(slot_selector, blocks)
    paired = match_gain * alive * (picked - flat_payload)
    reaction = spread_slots(slot_selector, paired)
    return (paired, reaction)


def per_device(disp, targets, stiffness, stiff_class, match_dest):
    field = disp[0]
    anchor = targets[0]
    row_count = field.shape[1]
    col_count = field.shape[2]
    block_count = row_count * (col_count // BLOCK)
    band_count = lax.axis_size("grid")
    capacity = max(2, 2 * block_count // band_count)
    member = (stiff_class[0][..., None] == jnp.arange(CLASSES)).astype(jnp.float32)
    kappa = jnp.repeat(jnp.sum(member * stiffness, axis=-1), BLOCK, axis=-1)
    marker = match_dest[0].reshape(block_count) + 1
    own_matrix, own_labels = placement(marker, block_count, band_count, capacity)
    velocity = jnp.zeros_like(field)
    for repeat_index in range(STEPS):
        extended = with_halo(field, (("grid", 1),), 1)
        blocks = field.reshape(2, block_count, BLOCK)
        pulled = (field - anchor).reshape(2, block_count, BLOCK)
        payload, labels = pack(pulled, own_matrix, own_labels, band_count, capacity)
        moved_payload, moved_labels = (
            lax.all_to_all(payload, "grid", split_axis=1, concat_axis=1, tiled=True),
            lax.all_to_all(labels, "grid", split_axis=1, concat_axis=1, tiled=True),
        )
        held_payload, held_labels = passed_along((moved_payload, moved_labels), "stack", 1)
        paired, reaction = settle(blocks, held_payload, held_labels)
        returned = passed_along(paired.reshape(2, band_count, capacity, BLOCK), "stack", -1)
        arrived = lax.all_to_all(returned, "grid", split_axis=1, concat_axis=1, tiled=True)
        gained = spread_slots(own_matrix, arrived.reshape(2, -1, BLOCK))
        match_force = (gained - reaction).reshape(2, row_count, col_count)
        velocity = damping * velocity + kappa * laplace(extended) + match_force
        field = field + velocity
    return (field[None], velocity[None])


TILE = 8
BAND = 256
VMEM_BYTES = 58 * 1024 * 1024


def two_pieces(value):
    high = value.astype(jnp.bfloat16)
    low = (value - high.astype(jnp.float32)).astype(jnp.bfloat16)
    return jnp.concatenate([high, low], axis=1)


def joined(pieces):
    return pieces[:, :BLOCK] + pieces[:, BLOCK:]


def relax_kernel(
    sections,
    bands,
    place_ref,
    data_ref,
    kappa_ref,
    dest_ref,
    dest_row_ref,
    out_ref,
    pick_ref,
    drop_ref,
    field_ref,
    velocity_ref,
    weight_ref,
    force_ref,
    pieces_ref,
    spread_ref,
    match_ref,
):
    total = bands * BAND
    lane = lax.broadcasted_iota(jnp.int32, (TILE, BLOCK), 1)
    sub = lax.broadcasted_iota(jnp.int32, (TILE, BLOCK), 0)
    section = place_ref[0]
    half = place_ref[1]

    def start_of(s, band):
        return data_ref[(band // 2) * sections + s, band % 2, 0]

    def target_of(s, band):
        return data_ref[(band // 2) * sections + s, band % 2, 1]

    def spread_band(slot, s, band):
        for k in range(BAND // TILE):
            centre = field_ref[s, band, k + 1]
            before = field_ref[s, band, k]
            after = field_ref[s, band, k + 2]
            left = pltpu.roll(jnp.where(lane == BLOCK - 1, before, centre), 1, 1)
            right = pltpu.roll(jnp.where(lane == 0, after, centre), BLOCK - 1, 1)
            spread_ref[slot, s, band + 1, k] = centre + 0.5 * (left + right)

    wide = lax.broadcasted_iota(jnp.int32, (BAND, BLOCK), 1)
    tall = lax.broadcasted_iota(jnp.int32, (BAND, BLOCK), 0)

    def build(band, carry):
        rows = pl.ds(pl.multiple_of(band * BAND, BAND), BAND)
        for s in range(sections - 1):
            dest = dest_ref[s, rows]
            for j in range(total // BLOCK):
                cols = slice(j * BLOCK, (j + 1) * BLOCK)
                hit = dest == wide + j * BLOCK
                pick_ref[s, rows, cols] = jnp.where(hit, 1.0, 0.0).astype(jnp.bfloat16)
                hit = dest_row_ref[s, :, cols] == tall + band * BAND
                drop_ref[s, rows, cols] = jnp.where(hit, 1.0, 0.0).astype(jnp.bfloat16)
        return carry

    lax.fori_loop(0, bands, build, 0)

    edge = jnp.zeros((BAND // TILE, TILE, BLOCK), jnp.float32)
    for s in range(sections):
        for slot in range(2):
            spread_ref[slot, s, 0] = edge
            spread_ref[slot, s, bands + 1] = edge

    def begin(band, carry):
        rows = pl.ds(pl.multiple_of(band * BAND, BAND), BAND)
        for s in range(sections):
            field_ref[s, band, 0] = edge[0]
            field_ref[s, band, BAND // TILE + 1] = edge[0]
            value = start_of(s, band)
            field_ref[s, band, 1 : BAND // TILE + 1] = value.reshape(BAND // TILE, TILE, BLOCK)
            pieces_ref[0, s, rows] = two_pieces(value)
            pieces_ref[1, s, rows] = two_pieces(target_of(s, band))
            velocity_ref[s, rows] = jnp.zeros((BAND, BLOCK), jnp.float32)
            spread_band(0, s, band)
        return carry

    lax.fori_loop(0, bands, begin, 0)

    ones = jnp.ones((total, BLOCK), jnp.bfloat16)

    def constants(band, carry):
        rows = pl.ds(pl.multiple_of(band * BAND, BAND), BAND)
        for s in range(sections):
            weight = 8.0 * kappa_ref[s, rows]
            force = jnp.zeros((BAND, BLOCK), jnp.float32)
            if s < sections - 1:
                alive = jnp.where(dest_ref[s, rows] >= 0, match_gain, 0.0)
                weight = weight + alive
                force = force + alive * target_of(s, band)
            if s > 0:
                drop = drop_ref[s - 1, rows]
                count = jnp.dot(drop, ones, preferred_element_type=jnp.float32)
                moved = jnp.dot(drop, pieces_ref[1, s - 1], preferred_element_type=jnp.float32)
                weight = weight + match_gain * count
                force = force - match_gain * joined(moved)
            weight_ref[s, rows] = weight
            force_ref[s, rows] = force
        return carry

    lax.fori_loop(0, bands, constants, 0)

    def step(t, carry):
        now = lax.rem(t, 2)
        later = 1 - now

        def one_section(s):
            def one_band(band, inner):
                rows = pl.ds(pl.multiple_of(band * BAND, BAND), BAND)
                sums = None
                if s < sections - 1:
                    sums = jnp.dot(
                        pick_ref[s, rows], pieces_ref[now, s + 1], preferred_element_type=jnp.float32
                    )
                if s > 0:
                    other = jnp.dot(
                        drop_ref[s - 1, rows],
                        pieces_ref[now, s - 1],
                        preferred_element_type=jnp.float32,
                    )
                    sums = other if sums is None else sums + other
                match_ref[...] = joined(sums)
                base = pl.multiple_of(band * BAND, BAND)
                for k in range(0, BAND // TILE, 2):
                    pair = []
                    for q in (k, k + 1):
                        spot = pl.ds(base + q * TILE, TILE)
                        here = spread_ref[now, s, band + 1, q]
                        above = spread_ref[now, s, band, q]
                        below = spread_ref[now, s, band + 2, q]
                        up = pltpu.roll(jnp.where(sub == TILE - 1, above, here), 1, 0)
                        down = pltpu.roll(jnp.where(sub == 0, below, here), TILE - 1, 0)
                        field = field_ref[s, band, q + 1]
                        velocity = (
                            damping * velocity_ref[s, spot]
                            + kappa_ref[s, spot] * (2.0 * here + up + down)
                            - weight_ref[s, spot] * field
                            + match_gain * match_ref[q * TILE : (q + 1) * TILE]
                            + force_ref[s, spot]
                        )
                        field = field + velocity
                        velocity_ref[s, spot] = velocity
                        field_ref[s, band, q + 1] = field
                        pair.append(field)
                    spot = pl.ds(base + k * TILE, 2 * TILE)
                    pieces_ref[later, s, spot] = two_pieces(jnp.concatenate(pair, axis=0))
                spread_band(later, s, band)
                return inner

            lax.fori_loop(0, bands, one_band, 0)

        for s in range(sections):
            distance = jnp.abs(section - s)

            @pl.when(distance <= STEPS - 1 - t)
            def _(s=s):
                one_section(s)

        return carry

    lax.fori_loop(0, STEPS, step, 0)
    for q in range(2):
        band = half * 2 + q
        out_ref[q, 0] = field_ref[section, band, 1 : BAND // TILE + 1].reshape(BAND, BLOCK)
        out_ref[q, 1] = velocity_ref[section, pl.ds(pl.multiple_of(band * BAND, BAND), BAND)]


def tiled_order(value):
    lead = value.shape[:-2]
    rows, cols = value.shape[-2:]
    split = value.reshape(*lead, rows, cols // BLOCK, BLOCK)
    return jnp.swapaxes(split, -3, -2).reshape(*lead, rows * (cols // BLOCK), BLOCK)


def whole_component(disp, targets, stiffness, stiff_class, match_dest):
    sections = lax.axis_size("stack")
    bands = lax.axis_size("half") * 2
    blocks_row = stiff_class.shape[-1]
    both = tiled_order(jnp.stack([disp[0], targets[0]], axis=1))
    both = lax.all_to_all(both, "comp", split_axis=0, concat_axis=0, tiled=True)
    data = lax.all_gather(both, ("half", "stack"))
    small = jnp.concatenate([stiff_class, match_dest])
    small = lax.all_gather(small, ("half", "comp", "stack"))
    small = small.reshape(bands, sections, 2, TILE, blocks_row).transpose(2, 1, 0, 4, 3)
    small = small.reshape(2, sections, bands * BAND)
    member = (small[0][..., None] == jnp.arange(CLASSES)).astype(jnp.float32)
    kappa = jnp.sum(member * stiffness, axis=-1)
    dest = small[1][: sections - 1]
    row, col = dest // blocks_row, dest % blocks_row
    dest = jnp.where(dest >= 0, (row // TILE) * BAND + col * TILE + row % TILE, -1)
    total = bands * BAND
    kappa_wide = jnp.broadcast_to(kappa[..., None], (sections, total, BLOCK))
    dest_wide = jnp.broadcast_to(dest[..., None], (sections - 1, total, BLOCK))
    place = jnp.stack([lax.axis_index("stack"), lax.axis_index("half")]).astype(jnp.int32)
    tiles = BAND // TILE
    result = pl.pallas_call(
        functools.partial(relax_kernel, sections, bands),
        out_shape=jax.ShapeDtypeStruct((2, 2, BAND, BLOCK), jnp.float32),
        in_specs=[pl.BlockSpec(memory_space=pltpu.SMEM)]
        + [pl.BlockSpec(memory_space=pltpu.VMEM)] * 4,
        out_specs=pl.BlockSpec(memory_space=pltpu.VMEM),
        scratch_shapes=[
            pltpu.VMEM((sections - 1, total, total), jnp.bfloat16),
            pltpu.VMEM((sections - 1, total, total), jnp.bfloat16),
            pltpu.VMEM((sections, bands, tiles + 2, TILE, BLOCK), jnp.float32),
            pltpu.VMEM((sections, total, BLOCK), jnp.float32),
            pltpu.VMEM((sections, total, BLOCK), jnp.float32),
            pltpu.VMEM((sections, total, BLOCK), jnp.float32),
            pltpu.VMEM((2, sections, total, 2 * BLOCK), jnp.bfloat16),
            pltpu.VMEM((2, sections, bands + 2, tiles, TILE, BLOCK), jnp.float32),
            pltpu.VMEM((BAND, BLOCK), jnp.float32),
        ],
        compiler_params=pltpu.CompilerParams(vmem_limit_bytes=VMEM_BYTES),
    )(place, data, kappa_wide, dest_wide, dest[:, None, :])
    result = lax.all_to_all(result, "comp", split_axis=0, concat_axis=0, tiled=True)
    result = result.reshape(2, 2, tiles, TILE, BLOCK).transpose(1, 0, 3, 2, 4)
    result = result.reshape(2, 1, 2, TILE, tiles * BLOCK)
    return (result[0], result[1])


def solution(mesh):
    by_name = mesh.shape
    if by_name["grid"] % 2 == 0 and by_name["grid"] <= 4 and by_name["stack"] <= 4:
        inner = Mesh(
            mesh.devices.reshape(by_name["slab"], by_name["grid"] // 2, 2, by_name["stack"]),
            ("slab", "half", "comp", "stack"),
        )
        body, grid = whole_component, ("half", "comp")
    else:
        inner, body, grid = mesh, per_device, "grid"
    return jax.shard_map(
        body,
        mesh=inner,
        in_specs=(
            P(("slab", "stack"), None, grid, None),
            P(("slab", "stack"), None, grid, None),
            P(),
            P(("slab", "stack"), grid, None),
            P(("slab", "stack"), grid, None),
        ),
        out_specs=(
            P(("slab", "stack"), None, grid, None),
            P(("slab", "stack"), None, grid, None),
        ),
        check_vma=False,
    )
```

```python
import functools

import jax
import jax.numpy as jnp
from jax import lax
from jax.experimental import pallas as pl
from jax.experimental.pallas import tpu as pltpu
from jax.sharding import Mesh
from jax.sharding import PartitionSpec as P

BLOCK = 128
CLASSES = 8
STEPS = 8


match_gain = 0.1
damping = 0.5


def with_halo(value, sides, width):
    for axis, dim in sides:
        peers, length = (lax.axis_size(axis), value.shape[dim])
        up = [(i, (i + 1) % peers) for i in range(peers - 1)]
        down = [(j, i) for i, j in up]
        last = lax.slice_in_dim(value, length - width, length, axis=dim)
        first = lax.slice_in_dim(value, 0, width, axis=dim)
        before = lax.ppermute(last, axis, up)
        after = lax.ppermute(first, axis, down)
        value = jnp.concatenate([before, value, after], axis=dim)
    return value


def passed_along(value, axis, steps):
    count = lax.axis_size(axis)
    first, last = (max(0, -steps), min(count, count - steps))
    return lax.ppermute(value, axis, [(source, source + steps) for source in range(first, last)])


def laplace(extended):
    padded = jnp.pad(extended, ((0, 0), (0, 0), (1, 1)))
    centre = padded[:, 1:-1, 1:-1]
    edge_sum = (
        padded[:, 2:, 1:-1] + padded[:, :-2, 1:-1] + padded[:, 1:-1, 2:] + padded[:, 1:-1, :-2]
    )
    corner_sum = padded[:, 2:, 2:] + padded[:, 2:, :-2] + padded[:, :-2, 2:] + padded[:, :-2, :-2]
    return edge_sum + 0.5 * corner_sum - 6.0 * centre


def placement(marker, block_count, band_count, capacity):
    alive = marker > 0
    target_block = jnp.maximum(marker - 1, 0)
    band_of = target_block // block_count
    member = ((band_of[:, None] == jnp.arange(band_count)[None, :]) & alive[:, None]).astype(
        jnp.int32
    )
    ranking = jnp.sum(jnp.cumsum(member, axis=0) * member, axis=1) - 1
    slot_of = jnp.where(alive, band_of * capacity + ranking, band_count * capacity)
    local_plus = jnp.where(alive, target_block % block_count + 1, 0)
    slot_total = band_count * capacity
    matching = slot_of[None, :] == jnp.arange(slot_total)[:, None]
    route_matrix = matching.astype(jnp.float32)
    labels = jnp.sum(jnp.where(matching, local_plus[None, :], 0), axis=1)
    return (route_matrix, labels)


def gather_slots(route_matrix, values):
    return jnp.einsum("sb,cbk->csk", route_matrix, values, precision=lax.Precision.HIGHEST)


def spread_slots(route_matrix, values):
    return jnp.einsum("sb,csk->cbk", route_matrix, values, precision=lax.Precision.HIGHEST)


def pack(values, route_matrix, labels, band_count, capacity):
    payload = gather_slots(route_matrix, values)
    return (
        payload.reshape(2, band_count, capacity, BLOCK),
        labels.reshape(1, band_count, capacity),
    )


def settle(blocks, payload, labels):
    block_count = blocks.shape[1]
    flat_payload = payload.reshape(2, -1, BLOCK)
    flat_labels = labels.reshape(-1)
    slot_selector = (flat_labels[:, None] - 1 == jnp.arange(block_count)[None, :]).astype(
        jnp.float32
    )
    alive = (flat_labels > 0).astype(jnp.float32)[None, :, None]
    picked = gather_slots(slot_selector, blocks)
    paired = match_gain * alive * (picked - flat_payload)
    reaction = spread_slots(slot_selector, paired)
    return (paired, reaction)


def per_device(disp, targets, stiffness, stiff_class, match_dest):
    field = disp[0]
    anchor = targets[0]
    row_count = field.shape[1]
    col_count = field.shape[2]
    block_count = row_count * (col_count // BLOCK)
    band_count = lax.axis_size("grid")
    capacity = max(2, 2 * block_count // band_count)
    member = (stiff_class[0][..., None] == jnp.arange(CLASSES)).astype(jnp.float32)
    kappa = jnp.repeat(jnp.sum(member * stiffness, axis=-1), BLOCK, axis=-1)
    marker = match_dest[0].reshape(block_count) + 1
    own_matrix, own_labels = placement(marker, block_count, band_count, capacity)
    velocity = jnp.zeros_like(field)
    for repeat_index in range(STEPS):
        extended = with_halo(field, (("grid", 1),), 1)
        blocks = field.reshape(2, block_count, BLOCK)
        pulled = (field - anchor).reshape(2, block_count, BLOCK)
        payload, labels = pack(pulled, own_matrix, own_labels, band_count, capacity)
        moved_payload, moved_labels = (
            lax.all_to_all(payload, "grid", split_axis=1, concat_axis=1, tiled=True),
            lax.all_to_all(labels, "grid", split_axis=1, concat_axis=1, tiled=True),
        )
        held_payload, held_labels = passed_along((moved_payload, moved_labels), "stack", 1)
        paired, reaction = settle(blocks, held_payload, held_labels)
        returned = passed_along(paired.reshape(2, band_count, capacity, BLOCK), "stack", -1)
        arrived = lax.all_to_all(returned, "grid", split_axis=1, concat_axis=1, tiled=True)
        gained = spread_slots(own_matrix, arrived.reshape(2, -1, BLOCK))
        match_force = (gained - reaction).reshape(2, row_count, col_count)
        velocity = damping * velocity + kappa * laplace(extended) + match_force
        field = field + velocity
    return (field[None], velocity[None])


TILE = 8
BAND = 256
VMEM_BYTES = 58 * 1024 * 1024


def two_pieces(value):
    high = value.astype(jnp.bfloat16)
    low = (value - high.astype(jnp.float32)).astype(jnp.bfloat16)
    return jnp.concatenate([high, low], axis=1)


def joined(pieces):
    return pieces[:, :BLOCK] + pieces[:, BLOCK:]


def relax_kernel(
    sections,
    bands,
    place_ref,
    data_ref,
    out_ref,
    kappa_ref,
    dest_ref,
    pick_ref,
    drop_ref,
    field_ref,
    velocity_ref,
    weight_ref,
    force_ref,
    pieces_ref,
    spread_ref,
    match_ref,
):
    total = bands * BAND
    lane = lax.broadcasted_iota(jnp.int32, (TILE, BLOCK), 1)
    sub = lax.broadcasted_iota(jnp.int32, (TILE, BLOCK), 0)
    section = place_ref[0]
    half = place_ref[1]

    def start_of(s, band):
        return data_ref[s // 2, s % 2, band, 0, 0:BAND]

    def target_of(s, band):
        return data_ref[s // 2, s % 2, band, 1, 0:BAND]

    def constant_row(s, which, j):
        line = BAND + 2 * which + j % 2
        return data_ref[s // 2, s % 2, j // 2, 0, line : line + 1]

    def as_column(row):
        return jnp.broadcast_to(row, (BLOCK, BLOCK)).T

    for s in range(sections):
        for j in range(total // BLOCK):
            spot = slice(j * BLOCK, (j + 1) * BLOCK)
            kappa_ref[s, spot] = as_column(constant_row(s, 0, j))
            if s < sections - 1:
                dest_ref[s, spot] = as_column(constant_row(s, 1, j)).astype(jnp.int32)

    def spread_band(slot, s, band):
        for k in range(BAND // TILE):
            centre = field_ref[s, band, k + 1]
            before = field_ref[s, band, k]
            after = field_ref[s, band, k + 2]
            left = pltpu.roll(jnp.where(lane == BLOCK - 1, before, centre), 1, 1)
            right = pltpu.roll(jnp.where(lane == 0, after, centre), BLOCK - 1, 1)
            spread_ref[slot, s, band + 1, k] = centre + 0.5 * (left + right)

    wide = lax.broadcasted_iota(jnp.int32, (BAND, BLOCK), 1)
    tall = lax.broadcasted_iota(jnp.int32, (BAND, BLOCK), 0)

    def build(band, carry):
        rows = pl.ds(pl.multiple_of(band * BAND, BAND), BAND)
        for s in range(sections - 1):
            dest = dest_ref[s, rows]
            for j in range(total // BLOCK):
                cols = slice(j * BLOCK, (j + 1) * BLOCK)
                hit = dest == wide + j * BLOCK
                pick_ref[s, rows, cols] = jnp.where(hit, 1.0, 0.0).astype(jnp.bfloat16)
                hit = constant_row(s, 1, j).astype(jnp.int32) == tall + band * BAND
                drop_ref[s, rows, cols] = jnp.where(hit, 1.0, 0.0).astype(jnp.bfloat16)
        return carry

    lax.fori_loop(0, bands, build, 0)

    edge = jnp.zeros((BAND // TILE, TILE, BLOCK), jnp.float32)
    for s in range(sections):
        for slot in range(2):
            spread_ref[slot, s, 0] = edge
            spread_ref[slot, s, bands + 1] = edge

    def begin(band, carry):
        rows = pl.ds(pl.multiple_of(band * BAND, BAND), BAND)
        for s in range(sections):
            field_ref[s, band, 0] = edge[0]
            field_ref[s, band, BAND // TILE + 1] = edge[0]
            value = start_of(s, band)
            field_ref[s, band, 1 : BAND // TILE + 1] = value.reshape(BAND // TILE, TILE, BLOCK)
            pieces_ref[0, s, rows] = two_pieces(value)
            pieces_ref[1, s, rows] = two_pieces(target_of(s, band))
            velocity_ref[s, rows] = jnp.zeros((BAND, BLOCK), jnp.float32)
            spread_band(0, s, band)
        return carry

    lax.fori_loop(0, bands, begin, 0)

    ones = jnp.ones((total, BLOCK), jnp.bfloat16)

    def constants(band, carry):
        rows = pl.ds(pl.multiple_of(band * BAND, BAND), BAND)
        for s in range(sections):
            weight = 8.0 * kappa_ref[s, rows]
            force = jnp.zeros((BAND, BLOCK), jnp.float32)
            if s < sections - 1:
                alive = jnp.where(dest_ref[s, rows] >= 0, match_gain, 0.0)
                weight = weight + alive
                force = force + alive * target_of(s, band)
            if s > 0:
                drop = drop_ref[s - 1, rows]
                count = jnp.dot(drop, ones, preferred_element_type=jnp.float32)
                moved = jnp.dot(drop, pieces_ref[1, s - 1], preferred_element_type=jnp.float32)
                weight = weight + match_gain * count
                force = force - match_gain * joined(moved)
            weight_ref[s, rows] = weight
            force_ref[s, rows] = force
        return carry

    lax.fori_loop(0, bands, constants, 0)

    def step(t, carry):
        now = lax.rem(t, 2)
        later = 1 - now

        def one_section(s):
            def one_band(band, inner):
                rows = pl.ds(pl.multiple_of(band * BAND, BAND), BAND)
                sums = None
                if s < sections - 1:
                    sums = jnp.dot(
                        pick_ref[s, rows], pieces_ref[now, s + 1], preferred_element_type=jnp.float32
                    )
                if s > 0:
                    other = jnp.dot(
                        drop_ref[s - 1, rows],
                        pieces_ref[now, s - 1],
                        preferred_element_type=jnp.float32,
                    )
                    sums = other if sums is None else sums + other
                match_ref[...] = joined(sums)
                base = pl.multiple_of(band * BAND, BAND)
                for k in range(0, BAND // TILE, 2):
                    pair = []
                    for q in (k, k + 1):
                        spot = pl.ds(base + q * TILE, TILE)
                        here = spread_ref[now, s, band + 1, q]
                        above = spread_ref[now, s, band, q]
                        below = spread_ref[now, s, band + 2, q]
                        up = pltpu.roll(jnp.where(sub == TILE - 1, above, here), 1, 0)
                        down = pltpu.roll(jnp.where(sub == 0, below, here), TILE - 1, 0)
                        field = field_ref[s, band, q + 1]
                        velocity = (
                            damping * velocity_ref[s, spot]
                            + kappa_ref[s, spot] * (2.0 * here + up + down)
                            - weight_ref[s, spot] * field
                            + match_gain * match_ref[q * TILE : (q + 1) * TILE]
                            + force_ref[s, spot]
                        )
                        field = field + velocity
                        velocity_ref[s, spot] = velocity
                        field_ref[s, band, q + 1] = field
                        pair.append(field)
                    spot = pl.ds(base + k * TILE, 2 * TILE)
                    pieces_ref[later, s, spot] = two_pieces(jnp.concatenate(pair, axis=0))
                spread_band(later, s, band)
                return inner

            lax.fori_loop(0, bands, one_band, 0)

        for s in range(sections):
            distance = jnp.abs(section - s)

            @pl.when(distance <= STEPS - 1 - t)
            def _(s=s):
                one_section(s)

        return carry

    lax.fori_loop(0, STEPS, step, 0)
    for q in range(2):
        band = half * 2 + q
        out_ref[q, 0] = field_ref[section, band, 1 : BAND // TILE + 1].reshape(BAND, BLOCK)
        out_ref[q, 1] = velocity_ref[section, pl.ds(pl.multiple_of(band * BAND, BAND), BAND)]


def tiled_order(value):
    lead = value.shape[:-2]
    rows, cols = value.shape[-2:]
    split = value.reshape(*lead, rows, cols // BLOCK, BLOCK)
    return jnp.swapaxes(split, -3, -2).reshape(*lead, rows * (cols // BLOCK), BLOCK)


def gather_kernel(bands, own_ref, data_ref, local_sem, send_sem, recv_sem):
    half, comp, stack = (lax.axis_index(name) for name in ("half", "comp", "stack"))
    slab = lax.axis_index("slab")
    z = half * 2 + comp
    x, core = stack // 2, stack % 2

    def device(to_x, to_core, to_z):
        return (slab, to_z // 2, to_z % 2, to_x * 2 + to_core)

    along = [lax.rem(z + j, bands) for j in range(bands)]
    over_x = device(1 - x, core, z)
    sibling = device(x, 1 - core, z)
    barrier = pltpu.get_barrier_semaphore()
    for peer in [device(x, core, to_z) for to_z in along[1:]] + [over_x, sibling]:
        pl.semaphore_signal(barrier, inc=1, device_id=peer, device_id_type=pl.DeviceIdType.MESH)
    pl.semaphore_wait(barrier, bands + 1)

    started = []

    def send(source, slot, kind, peer):
        copy = pltpu.make_async_remote_copy(
            src_ref=source,
            dst_ref=data_ref.at[slot],
            send_sem=send_sem.at[len(started)],
            recv_sem=recv_sem.at[slot],
            device_id=peer,
            device_id_type=pl.DeviceIdType.MESH,
        )
        copy.start()
        started.append(copy)

    def arrive(slot):
        pltpu.make_async_remote_copy(
            src_ref=data_ref.at[slot],
            dst_ref=data_ref.at[slot],
            send_sem=send_sem.at[0],
            recv_sem=recv_sem.at[slot],
            device_id=sibling,
            device_id_type=pl.DeviceIdType.MESH,
        ).wait_recv()

    for kind in range(2):
        for to_z in along[1:]:
            send(own_ref.at[to_z % 2, kind], (x, core, z, kind), kind, device(x, core, to_z))
        send(own_ref.at[comp, kind], (x, core, z, kind), kind, over_x)
        send(own_ref.at[comp, kind], (x, core, z, kind), kind, sibling)
        keep = pltpu.make_async_copy(
            own_ref.at[comp, kind], data_ref.at[x, core, z, kind], local_sem.at[kind]
        )
        keep.start()
    for kind in range(2):
        for band in along[1:]:
            slot = (x, core, band, kind)
            arrive(slot)
            send(data_ref.at[slot], slot, kind, over_x)
            send(data_ref.at[slot], slot, kind, sibling)
        for band in along:
            slot = (1 - x, core, band, kind)
            arrive(slot)
            send(data_ref.at[slot], slot, kind, sibling)
    for kind in range(2):
        for band in along:
            for from_x in range(2):
                arrive((from_x, 1 - core, band, kind))
    for copy in started:
        copy.wait_send()
    for kind in range(2):
        pltpu.make_async_copy(
            own_ref.at[comp, kind], data_ref.at[x, core, z, kind], local_sem.at[kind]
        ).wait()


def tiled_order(value):
    lead = value.shape[:-2]
    rows, cols = value.shape[-2:]
    split = value.reshape(*lead, rows, cols // BLOCK, BLOCK)
    return jnp.swapaxes(split, -3, -2).reshape(*lead, rows * (cols // BLOCK), BLOCK)


def whole_component(disp, targets, stiffness, stiff_class, match_dest):
    sections = lax.axis_size("stack")
    bands = lax.axis_size("half") * 2
    blocks_row = stiff_class.shape[-1]
    total = bands * BAND
    tiles = BAND // TILE
    member = (stiff_class[0][..., None] == jnp.arange(CLASSES)).astype(jnp.float32)
    kappa = jnp.sum(member * stiffness, axis=-1)
    dest = match_dest[0]
    row, col = dest // blocks_row, dest % blocks_row
    dest = jnp.where(dest >= 0, (row // TILE) * BAND + col * TILE + row % TILE, -1)
    constants = jnp.stack([kappa.T, dest.astype(jnp.float32).T]).reshape(4, BLOCK)
    constants = jnp.pad(constants, ((0, TILE - 4), (0, 0)))
    both = tiled_order(jnp.stack([disp[0], targets[0]], axis=1))
    extra = jnp.broadcast_to(constants, (2, 2, TILE, BLOCK))
    both = jnp.concatenate([both, extra], axis=2)
    copies = 2 * (bands + 1) + 2 * (2 * (bands - 1) + bands)
    data = pl.pallas_call(
        functools.partial(gather_kernel, bands),
        out_shape=jax.ShapeDtypeStruct(
            (sections // 2, 2, bands, 2, BAND + TILE, BLOCK), jnp.float32
        ),
        in_specs=[pl.BlockSpec(memory_space=pltpu.VMEM)],
        out_specs=pl.BlockSpec(memory_space=pltpu.VMEM),
        scratch_shapes=[
            pltpu.SemaphoreType.DMA((2,)),
            pltpu.SemaphoreType.DMA((copies,)),
            pltpu.SemaphoreType.DMA((sections // 2, 2, bands, 2)),
        ],
        compiler_params=pltpu.CompilerParams(
            collective_id=0, has_side_effects=True, vmem_limit_bytes=16 * 1024 * 1024
        ),
    )(both)
    place = jnp.stack([lax.axis_index("stack"), lax.axis_index("half")]).astype(jnp.int32)
    result = pl.pallas_call(
        functools.partial(relax_kernel, sections, bands),
        out_shape=jax.ShapeDtypeStruct((2, 2, BAND, BLOCK), jnp.float32),
        in_specs=[
            pl.BlockSpec(memory_space=pltpu.SMEM),
            pl.BlockSpec(memory_space=pltpu.VMEM),
        ],
        out_specs=pl.BlockSpec(memory_space=pltpu.VMEM),
        scratch_shapes=[
            pltpu.VMEM((sections, total, BLOCK), jnp.float32),
            pltpu.VMEM((sections - 1, total, BLOCK), jnp.int32),
            pltpu.VMEM((sections - 1, total, total), jnp.bfloat16),
            pltpu.VMEM((sections - 1, total, total), jnp.bfloat16),
            pltpu.VMEM((sections, bands, tiles + 2, TILE, BLOCK), jnp.float32),
            pltpu.VMEM((sections, total, BLOCK), jnp.float32),
            pltpu.VMEM((sections, total, BLOCK), jnp.float32),
            pltpu.VMEM((sections, total, BLOCK), jnp.float32),
            pltpu.VMEM((2, sections, total, 2 * BLOCK), jnp.bfloat16),
            pltpu.VMEM((2, sections, bands + 2, tiles, TILE, BLOCK), jnp.float32),
            pltpu.VMEM((BAND, BLOCK), jnp.float32),
        ],
        compiler_params=pltpu.CompilerParams(vmem_limit_bytes=VMEM_BYTES),
    )(place, data)
    result = lax.all_to_all(result, "comp", split_axis=0, concat_axis=0, tiled=True)
    result = result.reshape(2, 2, tiles, TILE, BLOCK).transpose(1, 0, 3, 2, 4)
    result = result.reshape(2, 1, 2, TILE, tiles * BLOCK)
    return (result[0], result[1])


def solution(mesh):
    by_name = mesh.shape
    if by_name["grid"] % 2 == 0 and by_name["grid"] <= 4 and by_name["stack"] == 4:
        inner = Mesh(
            mesh.devices.reshape(by_name["slab"], by_name["grid"] // 2, 2, by_name["stack"]),
            ("slab", "half", "comp", "stack"),
        )
        body, grid = whole_component, ("half", "comp")
    else:
        inner, body, grid = mesh, per_device, "grid"
    return jax.shard_map(
        body,
        mesh=inner,
        in_specs=(
            P(("slab", "stack"), None, grid, None),
            P(("slab", "stack"), None, grid, None),
            P(),
            P(("slab", "stack"), grid, None),
            P(("slab", "stack"), grid, None),
        ),
        out_specs=(
            P(("slab", "stack"), None, grid, None),
            P(("slab", "stack"), None, grid, None),
        ),
        check_vma=False,
    )
```

```python
import functools

import jax
import jax.numpy as jnp
from jax import lax
from jax.experimental import pallas as pl
from jax.experimental.pallas import tpu as pltpu
from jax.sharding import Mesh
from jax.sharding import PartitionSpec as P

BLOCK = 128
CLASSES = 8
STEPS = 8


match_gain = 0.1
damping = 0.5


def with_halo(value, sides, width):
    for axis, dim in sides:
        peers, length = (lax.axis_size(axis), value.shape[dim])
        up = [(i, (i + 1) % peers) for i in range(peers - 1)]
        down = [(j, i) for i, j in up]
        last = lax.slice_in_dim(value, length - width, length, axis=dim)
        first = lax.slice_in_dim(value, 0, width, axis=dim)
        before = lax.ppermute(last, axis, up)
        after = lax.ppermute(first, axis, down)
        value = jnp.concatenate([before, value, after], axis=dim)
    return value


def passed_along(value, axis, steps):
    count = lax.axis_size(axis)
    first, last = (max(0, -steps), min(count, count - steps))
    return lax.ppermute(value, axis, [(source, source + steps) for source in range(first, last)])


def laplace(extended):
    padded = jnp.pad(extended, ((0, 0), (0, 0), (1, 1)))
    centre = padded[:, 1:-1, 1:-1]
    edge_sum = (
        padded[:, 2:, 1:-1] + padded[:, :-2, 1:-1] + padded[:, 1:-1, 2:] + padded[:, 1:-1, :-2]
    )
    corner_sum = padded[:, 2:, 2:] + padded[:, 2:, :-2] + padded[:, :-2, 2:] + padded[:, :-2, :-2]
    return edge_sum + 0.5 * corner_sum - 6.0 * centre


def placement(marker, block_count, band_count, capacity):
    alive = marker > 0
    target_block = jnp.maximum(marker - 1, 0)
    band_of = target_block // block_count
    member = ((band_of[:, None] == jnp.arange(band_count)[None, :]) & alive[:, None]).astype(
        jnp.int32
    )
    ranking = jnp.sum(jnp.cumsum(member, axis=0) * member, axis=1) - 1
    slot_of = jnp.where(alive, band_of * capacity + ranking, band_count * capacity)
    local_plus = jnp.where(alive, target_block % block_count + 1, 0)
    slot_total = band_count * capacity
    matching = slot_of[None, :] == jnp.arange(slot_total)[:, None]
    route_matrix = matching.astype(jnp.float32)
    labels = jnp.sum(jnp.where(matching, local_plus[None, :], 0), axis=1)
    return (route_matrix, labels)


def gather_slots(route_matrix, values):
    return jnp.einsum("sb,cbk->csk", route_matrix, values, precision=lax.Precision.HIGHEST)


def spread_slots(route_matrix, values):
    return jnp.einsum("sb,csk->cbk", route_matrix, values, precision=lax.Precision.HIGHEST)


def pack(values, route_matrix, labels, band_count, capacity):
    payload = gather_slots(route_matrix, values)
    return (
        payload.reshape(2, band_count, capacity, BLOCK),
        labels.reshape(1, band_count, capacity),
    )


def settle(blocks, payload, labels):
    block_count = blocks.shape[1]
    flat_payload = payload.reshape(2, -1, BLOCK)
    flat_labels = labels.reshape(-1)
    slot_selector = (flat_labels[:, None] - 1 == jnp.arange(block_count)[None, :]).astype(
        jnp.float32
    )
    alive = (flat_labels > 0).astype(jnp.float32)[None, :, None]
    picked = gather_slots(slot_selector, blocks)
    paired = match_gain * alive * (picked - flat_payload)
    reaction = spread_slots(slot_selector, paired)
    return (paired, reaction)


def per_device(disp, targets, stiffness, stiff_class, match_dest):
    field = disp[0]
    anchor = targets[0]
    row_count = field.shape[1]
    col_count = field.shape[2]
    block_count = row_count * (col_count // BLOCK)
    band_count = lax.axis_size("grid")
    capacity = max(2, 2 * block_count // band_count)
    member = (stiff_class[0][..., None] == jnp.arange(CLASSES)).astype(jnp.float32)
    kappa = jnp.repeat(jnp.sum(member * stiffness, axis=-1), BLOCK, axis=-1)
    marker = match_dest[0].reshape(block_count) + 1
    own_matrix, own_labels = placement(marker, block_count, band_count, capacity)
    velocity = jnp.zeros_like(field)
    for repeat_index in range(STEPS):
        extended = with_halo(field, (("grid", 1),), 1)
        blocks = field.reshape(2, block_count, BLOCK)
        pulled = (field - anchor).reshape(2, block_count, BLOCK)
        payload, labels = pack(pulled, own_matrix, own_labels, band_count, capacity)
        moved_payload, moved_labels = (
            lax.all_to_all(payload, "grid", split_axis=1, concat_axis=1, tiled=True),
            lax.all_to_all(labels, "grid", split_axis=1, concat_axis=1, tiled=True),
        )
        held_payload, held_labels = passed_along((moved_payload, moved_labels), "stack", 1)
        paired, reaction = settle(blocks, held_payload, held_labels)
        returned = passed_along(paired.reshape(2, band_count, capacity, BLOCK), "stack", -1)
        arrived = lax.all_to_all(returned, "grid", split_axis=1, concat_axis=1, tiled=True)
        gained = spread_slots(own_matrix, arrived.reshape(2, -1, BLOCK))
        match_force = (gained - reaction).reshape(2, row_count, col_count)
        velocity = damping * velocity + kappa * laplace(extended) + match_force
        field = field + velocity
    return (field[None], velocity[None])


TILE = 8
BAND = 256
VMEM_BYTES = 58 * 1024 * 1024


def two_pieces(value):
    high = value.astype(jnp.bfloat16)
    low = (value - high.astype(jnp.float32)).astype(jnp.bfloat16)
    return jnp.concatenate([high, low], axis=1)


def joined(pieces):
    return pieces[:, :BLOCK] + pieces[:, BLOCK:]


def relax_kernel(
    bands,
    data_ref,
    out_ref,
    kappa_ref,
    out_of_inner_ref,
    in_of_outer_ref,
    in_of_far_ref,
    field_ref,
    velocity_ref,
    weight_ref,
    force_ref,
    pieces_ref,
    far_pieces_ref,
    far_ref,
    spread_ref,
    match_ref,
    swap_send,
    swap_recv,
    out_send,
    out_recv,
    out_local,
):
    total = bands * BAND
    tiles = BAND // TILE
    slab = lax.axis_index("slab")
    half, comp, stack = (lax.axis_index(name) for name in ("half", "comp", "stack"))
    z = half * 2 + comp
    other_z = half * 2 + 1 - comp
    x, core = stack // 2, stack % 2
    sections = (3 * core, 1 + core)
    far = 2 - core
    edge_source = 2 * core
    sibling = (slab, half, comp, x * 2 + 1 - core)
    beside = (slab, half, 1 - comp, x * 2 + core)
    across = (slab, half, 1 - comp, x * 2 + 1 - core)
    barrier = pltpu.get_barrier_semaphore()
    for peer in (sibling, beside, across):
        pl.semaphore_signal(barrier, inc=1, device_id=peer, device_id_type=pl.DeviceIdType.MESH)
    pl.semaphore_wait(barrier, 3)

    lane = lax.broadcasted_iota(jnp.int32, (TILE, BLOCK), 1)
    sub = lax.broadcasted_iota(jnp.int32, (TILE, BLOCK), 0)

    def loaded(s, band, kind):
        return data_ref[s // 2, s % 2, band, kind, 0:BAND]

    def constant_row(s, which, band, part):
        line = BAND + 2 * which + part
        return data_ref[s // 2, s % 2, band, 0, line : line + 1]

    def as_column(row):
        return jnp.broadcast_to(row, (BLOCK, BLOCK)).T

    def rows_of(band):
        return pl.ds(pl.multiple_of(band * BAND, BAND), BAND)

    def spread_band(slot, s, band):
        for k in range(tiles):
            centre = field_ref[s, band, k + 1]
            before = field_ref[s, band, k]
            after = field_ref[s, band, k + 2]
            left = pltpu.roll(jnp.where(lane == BLOCK - 1, before, centre), 1, 1)
            right = pltpu.roll(jnp.where(lane == 0, after, centre), BLOCK - 1, 1)
            spread_ref[slot, s, band + 1, k] = centre + 0.5 * (left + right)

    wide = lax.broadcasted_iota(jnp.int32, (BLOCK, BLOCK), 1).astype(jnp.float32)
    tall = lax.broadcasted_iota(jnp.int32, (BLOCK, BLOCK), 0).astype(jnp.float32)
    first = core == 0

    def build(band, carry):
        for part in range(2):
            base = band * BAND + part * BLOCK
            rows = pl.ds(pl.multiple_of(base, BLOCK), BLOCK)
            here = tall + base.astype(jnp.float32)
            for s in range(2):
                kappa_ref[s, rows] = as_column(constant_row(sections[s], 0, band, part))
            edge_column = as_column(constant_row(edge_source, 1, band, part))
            middle_column = as_column(constant_row(1, 1, band, part))
            for j in range(total // BLOCK):
                cols = slice(j * BLOCK, (j + 1) * BLOCK)
                there = wide + float(j * BLOCK)
                edge_row = constant_row(edge_source, 1, j // 2, j % 2)
                middle_row = constant_row(1, 1, j // 2, j % 2)
                pick = jnp.where(edge_column == there, 1.0, 0.0)
                drop = jnp.where(edge_row == here, 1.0, 0.0)
                out_of_inner_ref[rows, cols] = jnp.where(first, pick, drop).astype(jnp.bfloat16)
                in_of_outer_ref[rows, cols] = jnp.where(first, drop, pick).astype(jnp.bfloat16)
                pick = jnp.where(middle_column == there, 1.0, 0.0)
                drop = jnp.where(middle_row == here, 1.0, 0.0)
                in_of_far_ref[rows, cols] = jnp.where(first, pick, drop).astype(jnp.bfloat16)
        return carry

    lax.fori_loop(0, bands, build, 0)

    edge = jnp.zeros((tiles, TILE, BLOCK), jnp.float32)
    for s in range(2):
        for slot in range(2):
            spread_ref[slot, s, 0] = edge
            spread_ref[slot, s, bands + 1] = edge

    def begin(band, carry):
        rows = rows_of(band)
        for s in range(2):
            field_ref[s, band, 0] = edge[0]
            field_ref[s, band, tiles + 1] = edge[0]
            value = loaded(sections[s], band, 0)
            field_ref[s, band, 1 : tiles + 1] = value.reshape(tiles, TILE, BLOCK)
            pieces_ref[0, s, rows] = two_pieces(value)
            pieces_ref[1, s, rows] = two_pieces(loaded(sections[s], band, 1))
            velocity_ref[s, band] = edge
            spread_band(0, s, band)
        far_pieces_ref[rows] = two_pieces(loaded(far, band, 1))
        return carry

    lax.fori_loop(0, bands, begin, 0)

    ones = jnp.ones((total, BLOCK), jnp.bfloat16)

    def product(matrix, values):
        return jnp.dot(matrix, values, preferred_element_type=jnp.float32)

    def constants(band, carry):
        rows = rows_of(band)
        out_rows, in_rows, far_rows = (
            out_of_inner_ref[rows],
            in_of_outer_ref[rows],
            in_of_far_ref[rows],
        )
        count_out, count_in, count_far = (
            product(matrix, ones) for matrix in (out_rows, in_rows, far_rows)
        )
        weight_ref[0, rows] = 8.0 * kappa_ref[0, rows] + match_gain * count_out
        weight_ref[1, rows] = 8.0 * kappa_ref[1, rows] + match_gain * (count_in + count_far)
        ahead = count_out * loaded(sections[0], band, 1)
        behind = joined(product(out_rows, pieces_ref[1, 1]))
        force_ref[0, rows] = match_gain * jnp.where(first, ahead, -behind)
        alive = jnp.where(first, count_far, count_in)
        from_outer = joined(product(in_rows, pieces_ref[1, 0]))
        from_far = joined(product(far_rows, far_pieces_ref[...]))
        behind = jnp.where(first, from_outer, from_far)
        force_ref[1, rows] = match_gain * (alive * loaded(sections[1], band, 1) - behind)
        return carry

    lax.fori_loop(0, bands, constants, 0)

    def far_start(band, carry):
        far_pieces_ref[rows_of(band)] = two_pieces(loaded(far, band, 0))
        return carry

    lax.fori_loop(0, bands, far_start, 0)

    def swap(slot, band):
        return pltpu.make_async_remote_copy(
            src_ref=field_ref.at[1, band, pl.ds(1, tiles)],
            dst_ref=far_ref.at[slot, band],
            send_sem=swap_send.at[band],
            recv_sem=swap_recv.at[slot, band],
            device_id=sibling,
            device_id_type=pl.DeviceIdType.MESH,
        )

    def one_band(s, band, now, later):
        rows = rows_of(band)
        if s == 0:
            sums = product(out_of_inner_ref[rows], pieces_ref[now, 1])
        else:
            sums = product(in_of_outer_ref[rows], pieces_ref[now, 0])
            sums = sums + product(in_of_far_ref[rows], far_pieces_ref[...])
        match_ref[...] = joined(sums)
        base = pl.multiple_of(band * BAND, BAND)
        for k in range(0, tiles, 2):
            pair = []
            for q in (k, k + 1):
                spot = pl.ds(base + q * TILE, TILE)
                here = spread_ref[now, s, band + 1, q]
                above = spread_ref[now, s, band, q]
                below = spread_ref[now, s, band + 2, q]
                up = pltpu.roll(jnp.where(sub == TILE - 1, above, here), 1, 0)
                down = pltpu.roll(jnp.where(sub == 0, below, here), TILE - 1, 0)
                field = field_ref[s, band, q + 1]
                velocity = (
                    damping * velocity_ref[s, band, q]
                    + kappa_ref[s, spot] * (2.0 * here + up + down)
                    - weight_ref[s, spot] * field
                    + match_gain * match_ref[q * TILE : (q + 1) * TILE]
                    + force_ref[s, spot]
                )
                field = field + velocity
                velocity_ref[s, band, q] = velocity
                field_ref[s, band, q + 1] = field
                pair.append(field)
            spot = pl.ds(base + k * TILE, 2 * TILE)
            pieces_ref[later, s, spot] = two_pieces(jnp.concatenate(pair, axis=0))

    def step(t, carry):
        now = lax.rem(t, 2)
        later = 1 - now

        def inner(band, inside):
            one_band(1, band, now, later)
            swap(now, band).start()
            spread_band(later, 1, band)
            return inside

        def outer(band, inside):
            one_band(0, band, now, later)
            spread_band(later, 0, band)
            return inside

        lax.fori_loop(0, bands, inner, 0)
        lax.fori_loop(0, bands, outer, 0)

        def arrived(band, inside):
            swap(now, band).wait()
            value = far_ref[now, band].reshape(BAND, BLOCK)
            far_pieces_ref[rows_of(band)] = two_pieces(value)
            return inside

        lax.fori_loop(0, bands, arrived, 0)
        return carry

    lax.fori_loop(0, STEPS - 1, step, 0)

    now = (STEPS - 1) % 2
    sends = core == x

    def parts_of(s, band):
        return (field_ref.at[s, band, pl.ds(1, tiles)], velocity_ref.at[s, band])

    def deliver(s, band, peer, count):
        return [
            pltpu.make_async_remote_copy(
                src_ref=source,
                dst_ref=out_ref.at[comp, kind],
                send_sem=out_send.at[count, kind],
                recv_sem=out_recv.at[comp, kind],
                device_id=peer,
                device_id_type=pl.DeviceIdType.MESH,
            )
            for kind, source in enumerate(parts_of(s, band))
        ]

    def keep():
        return [
            pltpu.make_async_copy(source, out_ref.at[comp, kind], out_local.at[kind])
            for kind, source in enumerate(parts_of(0, z))
        ]

    def landed(which):
        return [
            pltpu.make_async_remote_copy(
                src_ref=out_ref.at[which, kind],
                dst_ref=out_ref.at[which, kind],
                send_sem=out_send.at[0, kind],
                recv_sem=out_recv.at[which, kind],
                device_id=sibling,
                device_id_type=pl.DeviceIdType.MESH,
            )
            for kind in range(2)
        ]

    @pl.when(sends)
    def _():
        one_band(1, other_z, now, 1 - now)
        for copy in deliver(1, other_z, across, 0):
            copy.start()
        one_band(0, other_z, now, 1 - now)
        for copy in deliver(0, other_z, beside, 1):
            copy.start()
        one_band(1, z, now, 1 - now)
        for copy in deliver(1, z, sibling, 2):
            copy.start()
        one_band(0, z, now, 1 - now)
        for copy in keep():
            copy.start()
        for copy in deliver(1, other_z, across, 0):
            copy.wait_send()
        for copy in deliver(0, other_z, beside, 1):
            copy.wait_send()
        for copy in deliver(1, z, sibling, 2):
            copy.wait_send()
        for copy in keep():
            copy.wait()

    @pl.when(jnp.logical_not(sends))
    def _():
        for copy in landed(comp):
            copy.wait_recv()

    for copy in landed(1 - comp):
        copy.wait_recv()


def gather_kernel(bands, own_ref, data_ref, local_sem, send_sem, recv_sem):
    half, comp, stack = (lax.axis_index(name) for name in ("half", "comp", "stack"))
    slab = lax.axis_index("slab")
    z = half * 2 + comp
    x, core = stack // 2, stack % 2

    def device(to_x, to_core, to_z):
        return (slab, to_z // 2, to_z % 2, to_x * 2 + to_core)

    along = [lax.rem(z + j, bands) for j in range(bands)]
    over_x = device(1 - x, core, z)
    sibling = device(x, 1 - core, z)
    barrier = pltpu.get_barrier_semaphore()
    for peer in [device(x, core, to_z) for to_z in along[1:]] + [over_x, sibling]:
        pl.semaphore_signal(barrier, inc=1, device_id=peer, device_id_type=pl.DeviceIdType.MESH)
    pl.semaphore_wait(barrier, bands + 1)

    started = []

    def send(source, slot, kind, peer):
        copy = pltpu.make_async_remote_copy(
            src_ref=source,
            dst_ref=data_ref.at[slot],
            send_sem=send_sem.at[len(started)],
            recv_sem=recv_sem.at[slot],
            device_id=peer,
            device_id_type=pl.DeviceIdType.MESH,
        )
        copy.start()
        started.append(copy)

    def arrive(slot):
        pltpu.make_async_remote_copy(
            src_ref=data_ref.at[slot],
            dst_ref=data_ref.at[slot],
            send_sem=send_sem.at[0],
            recv_sem=recv_sem.at[slot],
            device_id=sibling,
            device_id_type=pl.DeviceIdType.MESH,
        ).wait_recv()

    for kind in range(2):
        for to_z in along[1:]:
            send(own_ref.at[to_z % 2, kind], (x, core, z, kind), kind, device(x, core, to_z))
        send(own_ref.at[comp, kind], (x, core, z, kind), kind, over_x)
        send(own_ref.at[comp, kind], (x, core, z, kind), kind, sibling)
        keep = pltpu.make_async_copy(
            own_ref.at[comp, kind], data_ref.at[x, core, z, kind], local_sem.at[kind]
        )
        keep.start()
    for kind in range(2):
        for band in along[1:]:
            slot = (x, core, band, kind)
            arrive(slot)
            send(data_ref.at[slot], slot, kind, over_x)
            send(data_ref.at[slot], slot, kind, sibling)
        for band in along:
            slot = (1 - x, core, band, kind)
            arrive(slot)
            send(data_ref.at[slot], slot, kind, sibling)
    for kind in range(2):
        for band in along:
            for from_x in range(2):
                arrive((from_x, 1 - core, band, kind))
    for copy in started:
        copy.wait_send()
    for kind in range(2):
        pltpu.make_async_copy(
            own_ref.at[comp, kind], data_ref.at[x, core, z, kind], local_sem.at[kind]
        ).wait()


def tiled_order(value):
    lead = value.shape[:-2]
    rows, cols = value.shape[-2:]
    split = value.reshape(*lead, rows, cols // BLOCK, BLOCK)
    return jnp.swapaxes(split, -3, -2).reshape(*lead, rows * (cols // BLOCK), BLOCK)


def whole_component(disp, targets, stiffness, stiff_class, match_dest):
    sections = lax.axis_size("stack")
    bands = lax.axis_size("half") * 2
    blocks_row = stiff_class.shape[-1]
    total = bands * BAND
    tiles = BAND // TILE
    member = (stiff_class[0][..., None] == jnp.arange(CLASSES)).astype(jnp.float32)
    kappa = jnp.sum(member * stiffness, axis=-1)
    dest = match_dest[0]
    row, col = dest // blocks_row, dest % blocks_row
    dest = jnp.where(dest >= 0, (row // TILE) * BAND + col * TILE + row % TILE, -1)
    constants = jnp.stack([kappa.T, dest.astype(jnp.float32).T]).reshape(4, BLOCK)
    constants = jnp.pad(constants, ((0, TILE - 4), (0, 0)))
    both = tiled_order(jnp.stack([disp[0], targets[0]], axis=1))
    extra = jnp.broadcast_to(constants, (2, 2, TILE, BLOCK))
    both = jnp.concatenate([both, extra], axis=2)
    copies = 2 * (bands + 1) + 2 * (2 * (bands - 1) + bands)
    data = pl.pallas_call(
        functools.partial(gather_kernel, bands),
        out_shape=jax.ShapeDtypeStruct(
            (sections // 2, 2, bands, 2, BAND + TILE, BLOCK), jnp.float32
        ),
        in_specs=[pl.BlockSpec(memory_space=pltpu.VMEM)],
        out_specs=pl.BlockSpec(memory_space=pltpu.VMEM),
        scratch_shapes=[
            pltpu.SemaphoreType.DMA((2,)),
            pltpu.SemaphoreType.DMA((copies,)),
            pltpu.SemaphoreType.DMA((sections // 2, 2, bands, 2)),
        ],
        compiler_params=pltpu.CompilerParams(
            collective_id=0, has_side_effects=True, vmem_limit_bytes=16 * 1024 * 1024
        ),
    )(both)
    result = pl.pallas_call(
        functools.partial(relax_kernel, bands),
        out_shape=jax.ShapeDtypeStruct((2, 2, tiles, TILE, BLOCK), jnp.float32),
        in_specs=[pl.BlockSpec(memory_space=pltpu.VMEM)],
        out_specs=pl.BlockSpec(memory_space=pltpu.VMEM),
        scratch_shapes=[
            pltpu.VMEM((2, total, BLOCK), jnp.float32),
            pltpu.VMEM((total, total), jnp.bfloat16),
            pltpu.VMEM((total, total), jnp.bfloat16),
            pltpu.VMEM((total, total), jnp.bfloat16),
            pltpu.VMEM((2, bands, tiles + 2, TILE, BLOCK), jnp.float32),
            pltpu.VMEM((2, bands, tiles, TILE, BLOCK), jnp.float32),
            pltpu.VMEM((2, total, BLOCK), jnp.float32),
            pltpu.VMEM((2, total, BLOCK), jnp.float32),
            pltpu.VMEM((2, 2, total, 2 * BLOCK), jnp.bfloat16),
            pltpu.VMEM((total, 2 * BLOCK), jnp.bfloat16),
            pltpu.VMEM((2, bands, tiles, TILE, BLOCK), jnp.float32),
            pltpu.VMEM((2, 2, bands + 2, tiles, TILE, BLOCK), jnp.float32),
            pltpu.VMEM((BAND, BLOCK), jnp.float32),
            pltpu.SemaphoreType.DMA((bands,)),
            pltpu.SemaphoreType.DMA((2, bands)),
            pltpu.SemaphoreType.DMA((3, 2)),
            pltpu.SemaphoreType.DMA((2, 2)),
            pltpu.SemaphoreType.DMA((2,)),
        ],
        compiler_params=pltpu.CompilerParams(
            collective_id=1, has_side_effects=True, vmem_limit_bytes=VMEM_BYTES
        ),
    )(data)
    result = result.reshape(2, 2, tiles, TILE, BLOCK).transpose(1, 0, 3, 2, 4)
    result = result.reshape(2, 1, 2, TILE, tiles * BLOCK)
    return (result[0], result[1])


def solution(mesh):
    by_name = mesh.shape
    if by_name["grid"] % 2 == 0 and by_name["grid"] <= 4 and by_name["stack"] == 4:
        inner = Mesh(
            mesh.devices.reshape(by_name["slab"], by_name["grid"] // 2, 2, by_name["stack"]),
            ("slab", "half", "comp", "stack"),
        )
        body, grid = whole_component, ("half", "comp")
    else:
        inner, body, grid = mesh, per_device, "grid"
    return jax.shard_map(
        body,
        mesh=inner,
        in_specs=(
            P(("slab", "stack"), None, grid, None),
            P(("slab", "stack"), None, grid, None),
            P(),
            P(("slab", "stack"), grid, None),
            P(("slab", "stack"), grid, None),
        ),
        out_specs=(
            P(("slab", "stack"), None, grid, None),
            P(("slab", "stack"), None, grid, None),
        ),
        check_vma=False,
    )
```

```python
import functools

import jax
import jax.numpy as jnp
from jax import lax
from jax.experimental import pallas as pl
from jax.experimental.pallas import tpu as pltpu
from jax.sharding import Mesh
from jax.sharding import PartitionSpec as P

BLOCK = 128
CLASSES = 8
STEPS = 8


match_gain = 0.1
damping = 0.5


def with_halo(value, sides, width):
    for axis, dim in sides:
        peers, length = (lax.axis_size(axis), value.shape[dim])
        up = [(i, (i + 1) % peers) for i in range(peers - 1)]
        down = [(j, i) for i, j in up]
        last = lax.slice_in_dim(value, length - width, length, axis=dim)
        first = lax.slice_in_dim(value, 0, width, axis=dim)
        before = lax.ppermute(last, axis, up)
        after = lax.ppermute(first, axis, down)
        value = jnp.concatenate([before, value, after], axis=dim)
    return value


def passed_along(value, axis, steps):
    count = lax.axis_size(axis)
    first, last = (max(0, -steps), min(count, count - steps))
    return lax.ppermute(value, axis, [(source, source + steps) for source in range(first, last)])


def laplace(extended):
    padded = jnp.pad(extended, ((0, 0), (0, 0), (1, 1)))
    centre = padded[:, 1:-1, 1:-1]
    edge_sum = (
        padded[:, 2:, 1:-1] + padded[:, :-2, 1:-1] + padded[:, 1:-1, 2:] + padded[:, 1:-1, :-2]
    )
    corner_sum = padded[:, 2:, 2:] + padded[:, 2:, :-2] + padded[:, :-2, 2:] + padded[:, :-2, :-2]
    return edge_sum + 0.5 * corner_sum - 6.0 * centre


def placement(marker, block_count, band_count, capacity):
    alive = marker > 0
    target_block = jnp.maximum(marker - 1, 0)
    band_of = target_block // block_count
    member = ((band_of[:, None] == jnp.arange(band_count)[None, :]) & alive[:, None]).astype(
        jnp.int32
    )
    ranking = jnp.sum(jnp.cumsum(member, axis=0) * member, axis=1) - 1
    slot_of = jnp.where(alive, band_of * capacity + ranking, band_count * capacity)
    local_plus = jnp.where(alive, target_block % block_count + 1, 0)
    slot_total = band_count * capacity
    matching = slot_of[None, :] == jnp.arange(slot_total)[:, None]
    route_matrix = matching.astype(jnp.float32)
    labels = jnp.sum(jnp.where(matching, local_plus[None, :], 0), axis=1)
    return (route_matrix, labels)


def gather_slots(route_matrix, values):
    return jnp.einsum("sb,cbk->csk", route_matrix, values, precision=lax.Precision.HIGHEST)


def spread_slots(route_matrix, values):
    return jnp.einsum("sb,csk->cbk", route_matrix, values, precision=lax.Precision.HIGHEST)


def pack(values, route_matrix, labels, band_count, capacity):
    payload = gather_slots(route_matrix, values)
    return (
        payload.reshape(2, band_count, capacity, BLOCK),
        labels.reshape(1, band_count, capacity),
    )


def settle(blocks, payload, labels):
    block_count = blocks.shape[1]
    flat_payload = payload.reshape(2, -1, BLOCK)
    flat_labels = labels.reshape(-1)
    slot_selector = (flat_labels[:, None] - 1 == jnp.arange(block_count)[None, :]).astype(
        jnp.float32
    )
    alive = (flat_labels > 0).astype(jnp.float32)[None, :, None]
    picked = gather_slots(slot_selector, blocks)
    paired = match_gain * alive * (picked - flat_payload)
    reaction = spread_slots(slot_selector, paired)
    return (paired, reaction)


def per_device(disp, targets, stiffness, stiff_class, match_dest):
    field = disp[0]
    anchor = targets[0]
    row_count = field.shape[1]
    col_count = field.shape[2]
    block_count = row_count * (col_count // BLOCK)
    band_count = lax.axis_size("grid")
    capacity = max(2, 2 * block_count // band_count)
    member = (stiff_class[0][..., None] == jnp.arange(CLASSES)).astype(jnp.float32)
    kappa = jnp.repeat(jnp.sum(member * stiffness, axis=-1), BLOCK, axis=-1)
    marker = match_dest[0].reshape(block_count) + 1
    own_matrix, own_labels = placement(marker, block_count, band_count, capacity)
    velocity = jnp.zeros_like(field)
    for repeat_index in range(STEPS):
        extended = with_halo(field, (("grid", 1),), 1)
        blocks = field.reshape(2, block_count, BLOCK)
        pulled = (field - anchor).reshape(2, block_count, BLOCK)
        payload, labels = pack(pulled, own_matrix, own_labels, band_count, capacity)
        moved_payload, moved_labels = (
            lax.all_to_all(payload, "grid", split_axis=1, concat_axis=1, tiled=True),
            lax.all_to_all(labels, "grid", split_axis=1, concat_axis=1, tiled=True),
        )
        held_payload, held_labels = passed_along((moved_payload, moved_labels), "stack", 1)
        paired, reaction = settle(blocks, held_payload, held_labels)
        returned = passed_along(paired.reshape(2, band_count, capacity, BLOCK), "stack", -1)
        arrived = lax.all_to_all(returned, "grid", split_axis=1, concat_axis=1, tiled=True)
        gained = spread_slots(own_matrix, arrived.reshape(2, -1, BLOCK))
        match_force = (gained - reaction).reshape(2, row_count, col_count)
        velocity = damping * velocity + kappa * laplace(extended) + match_force
        field = field + velocity
    return (field[None], velocity[None])


TILE = 8
BAND = 256
VMEM_BYTES = 58 * 1024 * 1024


def two_pieces(value):
    high = value.astype(jnp.bfloat16)
    low = (value - high.astype(jnp.float32)).astype(jnp.bfloat16)
    return jnp.concatenate([high, low], axis=1)


def joined(pieces):
    return pieces[:, :BLOCK] + pieces[:, BLOCK:]


def relax_kernel(
    bands,
    own_ref,
    out_ref,
    data_ref,
    kappa_ref,
    out_of_inner_ref,
    in_of_outer_ref,
    in_of_far_ref,
    field_ref,
    velocity_ref,
    weight_ref,
    force_ref,
    pieces_ref,
    far_pieces_ref,
    far_ref,
    spread_ref,
    match_ref,
    swap_send,
    swap_recv,
    out_send,
    out_recv,
    out_local,
    local_sem,
    send_sem,
    recv_sem,
):
    total = bands * BAND
    tiles = BAND // TILE
    slab = lax.axis_index("slab")
    half, comp, stack = (lax.axis_index(name) for name in ("half", "comp", "stack"))
    z = half * 2 + comp
    other_z = half * 2 + 1 - comp
    x, core = stack // 2, stack % 2
    sections = (3 * core, 1 + core)
    far = 2 - core
    edge_source = 2 * core
    sibling = (slab, half, comp, x * 2 + 1 - core)
    beside = (slab, half, 1 - comp, x * 2 + core)
    across = (slab, half, 1 - comp, x * 2 + 1 - core)
    barrier = pltpu.get_barrier_semaphore()
    over_x = (slab, half, comp, (1 - x) * 2 + core)
    along = [other_z, 2 - half, 3 - 3 * half]

    def column(to_z):
        return (slab, to_z // 2, to_z % 2, stack)

    for peer in [column(to_z) for to_z in along] + [sibling, across, over_x]:
        pl.semaphore_signal(barrier, inc=1, device_id=peer, device_id_type=pl.DeviceIdType.MESH)
    pl.semaphore_wait(barrier, 6)

    started = []

    def send(source, slot, peer):
        copy = pltpu.make_async_remote_copy(
            src_ref=source,
            dst_ref=data_ref.at[slot],
            send_sem=send_sem.at[len(started)],
            recv_sem=recv_sem.at[slot],
            device_id=peer,
            device_id_type=pl.DeviceIdType.MESH,
        )
        copy.start()
        started.append(copy)

    def arrive(slot):
        pltpu.make_async_remote_copy(
            src_ref=data_ref.at[slot],
            dst_ref=data_ref.at[slot],
            send_sem=send_sem.at[0],
            recv_sem=recv_sem.at[slot],
            device_id=sibling,
            device_id_type=pl.DeviceIdType.MESH,
        ).wait_recv()

    kept = []
    for kind in range(2):
        for to_z in along:
            send(own_ref.at[to_z % 2, kind], (x, core, z, kind), column(to_z))
        send(own_ref.at[comp, kind], (x, core, z, kind), over_x)
        copy = pltpu.make_async_copy(
            own_ref.at[comp, kind], data_ref.at[x, core, z, kind], local_sem.at[kind]
        )
        copy.start()
        kept.append(copy)
    for copy in kept:
        copy.wait()

    def forward_column(kind):
        for band in along:
            slot = (x, core, band, kind)
            arrive(slot)
            send(data_ref.at[slot], slot, over_x)

    def forward_sibling(kind):
        for band in [z] + along:
            arrive((1 - x, core, band, kind))
        for band in [z] + along:
            slot = (1 - core, core, band, kind)
            send(data_ref.at[slot], slot, sibling)

    def from_sibling(kind):
        for band in [z] + along:
            arrive((core, 1 - core, band, kind))

    forward_column(0)
    forward_sibling(0)
    forward_column(1)
    from_sibling(0)

    lane = lax.broadcasted_iota(jnp.int32, (TILE, BLOCK), 1)
    sub = lax.broadcasted_iota(jnp.int32, (TILE, BLOCK), 0)

    def loaded(s, band, kind):
        return data_ref[s // 2, s % 2, band, kind, 0:BAND]

    def constant_row(s, which, band, part):
        line = BAND + 2 * which + part
        return data_ref[s // 2, s % 2, band, 0, line : line + 1]

    def as_column(row):
        return jnp.broadcast_to(row, (BLOCK, BLOCK)).T

    def rows_of(band):
        return pl.ds(pl.multiple_of(band * BAND, BAND), BAND)

    def spread_band(slot, s, band):
        for k in range(tiles):
            centre = field_ref[s, band, k + 1]
            before = field_ref[s, band, k]
            after = field_ref[s, band, k + 2]
            left = pltpu.roll(jnp.where(lane == BLOCK - 1, before, centre), 1, 1)
            right = pltpu.roll(jnp.where(lane == 0, after, centre), BLOCK - 1, 1)
            spread_ref[slot, s, band + 1, k] = centre + 0.5 * (left + right)

    wide = lax.broadcasted_iota(jnp.int32, (BLOCK, BLOCK), 1).astype(jnp.float32)
    tall = lax.broadcasted_iota(jnp.int32, (BLOCK, BLOCK), 0).astype(jnp.float32)
    first = core == 0

    def build(band, carry):
        for part in range(2):
            base = band * BAND + part * BLOCK
            rows = pl.ds(pl.multiple_of(base, BLOCK), BLOCK)
            here = tall + base.astype(jnp.float32)
            for s in range(2):
                kappa_ref[s, rows] = as_column(constant_row(sections[s], 0, band, part))
            edge_column = as_column(constant_row(edge_source, 1, band, part))
            middle_column = as_column(constant_row(1, 1, band, part))
            for j in range(total // BLOCK):
                cols = slice(j * BLOCK, (j + 1) * BLOCK)
                there = wide + float(j * BLOCK)
                edge_row = constant_row(edge_source, 1, j // 2, j % 2)
                middle_row = constant_row(1, 1, j // 2, j % 2)
                pick = jnp.where(edge_column == there, 1.0, 0.0)
                drop = jnp.where(edge_row == here, 1.0, 0.0)
                out_of_inner_ref[rows, cols] = jnp.where(first, pick, drop).astype(jnp.bfloat16)
                in_of_outer_ref[rows, cols] = jnp.where(first, drop, pick).astype(jnp.bfloat16)
                pick = jnp.where(middle_column == there, 1.0, 0.0)
                drop = jnp.where(middle_row == here, 1.0, 0.0)
                in_of_far_ref[rows, cols] = jnp.where(first, pick, drop).astype(jnp.bfloat16)
        return carry

    lax.fori_loop(0, bands, build, 0)

    edge = jnp.zeros((tiles, TILE, BLOCK), jnp.float32)
    for s in range(2):
        for slot in range(2):
            spread_ref[slot, s, 0] = edge
            spread_ref[slot, s, bands + 1] = edge

    def begin(band, carry):
        rows = rows_of(band)
        for s in range(2):
            field_ref[s, band, 0] = edge[0]
            field_ref[s, band, tiles + 1] = edge[0]
            value = loaded(sections[s], band, 0)
            field_ref[s, band, 1 : tiles + 1] = value.reshape(tiles, TILE, BLOCK)
            pieces_ref[0, s, rows] = two_pieces(value)
            velocity_ref[s, band] = edge
            spread_band(0, s, band)
        return carry

    lax.fori_loop(0, bands, begin, 0)

    forward_sibling(1)
    from_sibling(1)

    def offsets(band, carry):
        rows = rows_of(band)
        for s in range(2):
            pieces_ref[1, s, rows] = two_pieces(loaded(sections[s], band, 1))
        far_pieces_ref[rows] = two_pieces(loaded(far, band, 1))
        return carry

    lax.fori_loop(0, bands, offsets, 0)

    ones = jnp.ones((total, BLOCK), jnp.bfloat16)

    def product(matrix, values):
        return jnp.dot(matrix, values, preferred_element_type=jnp.float32)

    def constants(band, carry):
        rows = rows_of(band)
        out_rows, in_rows, far_rows = (
            out_of_inner_ref[rows],
            in_of_outer_ref[rows],
            in_of_far_ref[rows],
        )
        count_out, count_in, count_far = (
            product(matrix, ones) for matrix in (out_rows, in_rows, far_rows)
        )
        weight_ref[0, rows] = 8.0 * kappa_ref[0, rows] + match_gain * count_out
        weight_ref[1, rows] = 8.0 * kappa_ref[1, rows] + match_gain * (count_in + count_far)
        ahead = count_out * loaded(sections[0], band, 1)
        behind = joined(product(out_rows, pieces_ref[1, 1]))
        force_ref[0, rows] = match_gain * jnp.where(first, ahead, -behind)
        alive = jnp.where(first, count_far, count_in)
        from_outer = joined(product(in_rows, pieces_ref[1, 0]))
        from_far = joined(product(far_rows, far_pieces_ref[...]))
        behind = jnp.where(first, from_outer, from_far)
        force_ref[1, rows] = match_gain * (alive * loaded(sections[1], band, 1) - behind)
        return carry

    lax.fori_loop(0, bands, constants, 0)

    def far_start(band, carry):
        far_pieces_ref[rows_of(band)] = two_pieces(loaded(far, band, 0))
        return carry

    lax.fori_loop(0, bands, far_start, 0)

    def swap(slot, band):
        return pltpu.make_async_remote_copy(
            src_ref=field_ref.at[1, band, pl.ds(1, tiles)],
            dst_ref=far_ref.at[slot, band],
            send_sem=swap_send.at[band],
            recv_sem=swap_recv.at[slot, band],
            device_id=sibling,
            device_id_type=pl.DeviceIdType.MESH,
        )

    def one_band(s, band, now, later):
        rows = rows_of(band)
        if s == 0:
            sums = product(out_of_inner_ref[rows], pieces_ref[now, 1])
        else:
            sums = product(in_of_outer_ref[rows], pieces_ref[now, 0])
            sums = sums + product(in_of_far_ref[rows], far_pieces_ref[...])
        match_ref[...] = joined(sums)
        base = pl.multiple_of(band * BAND, BAND)
        for k in range(0, tiles, 2):
            pair = []
            for q in (k, k + 1):
                spot = pl.ds(base + q * TILE, TILE)
                here = spread_ref[now, s, band + 1, q]
                above = spread_ref[now, s, band, q]
                below = spread_ref[now, s, band + 2, q]
                up = pltpu.roll(jnp.where(sub == TILE - 1, above, here), 1, 0)
                down = pltpu.roll(jnp.where(sub == 0, below, here), TILE - 1, 0)
                field = field_ref[s, band, q + 1]
                velocity = (
                    damping * velocity_ref[s, band, q]
                    + kappa_ref[s, spot] * (2.0 * here + up + down)
                    - weight_ref[s, spot] * field
                    + match_gain * match_ref[q * TILE : (q + 1) * TILE]
                    + force_ref[s, spot]
                )
                field = field + velocity
                velocity_ref[s, band, q] = velocity
                field_ref[s, band, q + 1] = field
                pair.append(field)
            spot = pl.ds(base + k * TILE, 2 * TILE)
            pieces_ref[later, s, spot] = two_pieces(jnp.concatenate(pair, axis=0))

    def step(t, carry):
        now = lax.rem(t, 2)
        later = 1 - now

        def inner(band, inside):
            one_band(1, band, now, later)
            swap(now, band).start()
            spread_band(later, 1, band)
            return inside

        def outer(band, inside):
            one_band(0, band, now, later)
            spread_band(later, 0, band)
            return inside

        lax.fori_loop(0, bands, inner, 0)
        lax.fori_loop(0, bands, outer, 0)

        def arrived(band, inside):
            swap(now, band).wait()
            value = far_ref[now, band].reshape(BAND, BLOCK)
            far_pieces_ref[rows_of(band)] = two_pieces(value)
            return inside

        lax.fori_loop(0, bands, arrived, 0)
        return carry

    lax.fori_loop(0, STEPS - 1, step, 0)

    now = (STEPS - 1) % 2
    sends = core == x

    def parts_of(s, band):
        return (field_ref.at[s, band, pl.ds(1, tiles)], velocity_ref.at[s, band])

    def deliver(s, band, peer, count):
        return [
            pltpu.make_async_remote_copy(
                src_ref=source,
                dst_ref=out_ref.at[comp, kind],
                send_sem=out_send.at[count, kind],
                recv_sem=out_recv.at[comp, kind],
                device_id=peer,
                device_id_type=pl.DeviceIdType.MESH,
            )
            for kind, source in enumerate(parts_of(s, band))
        ]

    def keep():
        return [
            pltpu.make_async_copy(source, out_ref.at[comp, kind], out_local.at[kind])
            for kind, source in enumerate(parts_of(0, z))
        ]

    def landed(which):
        return [
            pltpu.make_async_remote_copy(
                src_ref=out_ref.at[which, kind],
                dst_ref=out_ref.at[which, kind],
                send_sem=out_send.at[0, kind],
                recv_sem=out_recv.at[which, kind],
                device_id=sibling,
                device_id_type=pl.DeviceIdType.MESH,
            )
            for kind in range(2)
        ]

    @pl.when(sends)
    def _():
        one_band(1, other_z, now, 1 - now)
        for copy in deliver(1, other_z, across, 0):
            copy.start()
        one_band(0, other_z, now, 1 - now)
        for copy in deliver(0, other_z, beside, 1):
            copy.start()
        one_band(1, z, now, 1 - now)
        for copy in deliver(1, z, sibling, 2):
            copy.start()
        one_band(0, z, now, 1 - now)
        for copy in keep():
            copy.start()
        for copy in deliver(1, other_z, across, 0):
            copy.wait_send()
        for copy in deliver(0, other_z, beside, 1):
            copy.wait_send()
        for copy in deliver(1, z, sibling, 2):
            copy.wait_send()
        for copy in keep():
            copy.wait()

    @pl.when(jnp.logical_not(sends))
    def _():
        for copy in landed(comp):
            copy.wait_recv()

    for copy in landed(1 - comp):
        copy.wait_recv()
    for copy in started:
        copy.wait_send()


def tiled_order(value):
    lead = value.shape[:-2]
    rows, cols = value.shape[-2:]
    split = value.reshape(*lead, rows, cols // BLOCK, BLOCK)
    return jnp.swapaxes(split, -3, -2).reshape(*lead, rows * (cols // BLOCK), BLOCK)


def whole_component(disp, targets, stiffness, stiff_class, match_dest):
    sections = lax.axis_size("stack")
    bands = lax.axis_size("half") * 2
    blocks_row = stiff_class.shape[-1]
    total = bands * BAND
    tiles = BAND // TILE
    member = (stiff_class[0][..., None] == jnp.arange(CLASSES)).astype(jnp.float32)
    kappa = jnp.sum(member * stiffness, axis=-1)
    dest = match_dest[0]
    row, col = dest // blocks_row, dest % blocks_row
    dest = jnp.where(dest >= 0, (row // TILE) * BAND + col * TILE + row % TILE, -1)
    constants = jnp.stack([kappa.T, dest.astype(jnp.float32).T]).reshape(4, BLOCK)
    constants = jnp.pad(constants, ((0, TILE - 4), (0, 0)))
    both = tiled_order(jnp.stack([disp[0], targets[0]], axis=1))
    extra = jnp.broadcast_to(constants, (2, 2, TILE, BLOCK))
    both = jnp.concatenate([both, extra], axis=2)
    result = pl.pallas_call(
        functools.partial(relax_kernel, bands),
        out_shape=jax.ShapeDtypeStruct((2, 2, tiles, TILE, BLOCK), jnp.float32),
        in_specs=[pl.BlockSpec(memory_space=pltpu.VMEM)],
        out_specs=pl.BlockSpec(memory_space=pltpu.VMEM),
        scratch_shapes=[
            pltpu.VMEM((sections // 2, 2, bands, 2, BAND + TILE, BLOCK), jnp.float32),
            pltpu.VMEM((2, total, BLOCK), jnp.float32),
            pltpu.VMEM((total, total), jnp.bfloat16),
            pltpu.VMEM((total, total), jnp.bfloat16),
            pltpu.VMEM((total, total), jnp.bfloat16),
            pltpu.VMEM((2, bands, tiles + 2, TILE, BLOCK), jnp.float32),
            pltpu.VMEM((2, bands, tiles, TILE, BLOCK), jnp.float32),
            pltpu.VMEM((2, total, BLOCK), jnp.float32),
            pltpu.VMEM((2, total, BLOCK), jnp.float32),
            pltpu.VMEM((2, 2, total, 2 * BLOCK), jnp.bfloat16),
            pltpu.VMEM((total, 2 * BLOCK), jnp.bfloat16),
            pltpu.VMEM((2, bands, tiles, TILE, BLOCK), jnp.float32),
            pltpu.VMEM((2, 2, bands + 2, tiles, TILE, BLOCK), jnp.float32),
            pltpu.VMEM((BAND, BLOCK), jnp.float32),
            pltpu.SemaphoreType.DMA((bands,)),
            pltpu.SemaphoreType.DMA((2, bands)),
            pltpu.SemaphoreType.DMA((3, 2)),
            pltpu.SemaphoreType.DMA((2, 2)),
            pltpu.SemaphoreType.DMA((2,)),
            pltpu.SemaphoreType.DMA((2,)),
            pltpu.SemaphoreType.DMA((22,)),
            pltpu.SemaphoreType.DMA((sections // 2, 2, bands, 2)),
        ],
        compiler_params=pltpu.CompilerParams(
            collective_id=0, has_side_effects=True, vmem_limit_bytes=VMEM_BYTES
        ),
    )(both)
    result = result.reshape(2, 2, tiles, TILE, BLOCK).transpose(1, 0, 3, 2, 4)
    result = result.reshape(2, 1, 2, TILE, tiles * BLOCK)
    return (result[0], result[1])


def solution(mesh):
    by_name = mesh.shape
    if by_name["grid"] == 4 and by_name["stack"] == 4:
        inner = Mesh(
            mesh.devices.reshape(by_name["slab"], by_name["grid"] // 2, 2, by_name["stack"]),
            ("slab", "half", "comp", "stack"),
        )
        body, grid = whole_component, ("half", "comp")
    else:
        inner, body, grid = mesh, per_device, "grid"
    return jax.shard_map(
        body,
        mesh=inner,
        in_specs=(
            P(("slab", "stack"), None, grid, None),
            P(("slab", "stack"), None, grid, None),
            P(),
            P(("slab", "stack"), grid, None),
            P(("slab", "stack"), grid, None),
        ),
        out_specs=(
            P(("slab", "stack"), None, grid, None),
            P(("slab", "stack"), None, grid, None),
        ),
        check_vma=False,
    )
```

```python
import functools

import jax
import jax.numpy as jnp
from jax import lax
from jax.experimental import pallas as pl
from jax.experimental.pallas import tpu as pltpu
from jax.sharding import Mesh
from jax.sharding import PartitionSpec as P

BLOCK = 128
CLASSES = 8
STEPS = 8


match_gain = 0.1
damping = 0.5


def with_halo(value, sides, width):
    for axis, dim in sides:
        peers, length = (lax.axis_size(axis), value.shape[dim])
        up = [(i, (i + 1) % peers) for i in range(peers - 1)]
        down = [(j, i) for i, j in up]
        last = lax.slice_in_dim(value, length - width, length, axis=dim)
        first = lax.slice_in_dim(value, 0, width, axis=dim)
        before = lax.ppermute(last, axis, up)
        after = lax.ppermute(first, axis, down)
        value = jnp.concatenate([before, value, after], axis=dim)
    return value


def passed_along(value, axis, steps):
    count = lax.axis_size(axis)
    first, last = (max(0, -steps), min(count, count - steps))
    return lax.ppermute(value, axis, [(source, source + steps) for source in range(first, last)])


def laplace(extended):
    padded = jnp.pad(extended, ((0, 0), (0, 0), (1, 1)))
    centre = padded[:, 1:-1, 1:-1]
    edge_sum = (
        padded[:, 2:, 1:-1] + padded[:, :-2, 1:-1] + padded[:, 1:-1, 2:] + padded[:, 1:-1, :-2]
    )
    corner_sum = padded[:, 2:, 2:] + padded[:, 2:, :-2] + padded[:, :-2, 2:] + padded[:, :-2, :-2]
    return edge_sum + 0.5 * corner_sum - 6.0 * centre


def placement(marker, block_count, band_count, capacity):
    alive = marker > 0
    target_block = jnp.maximum(marker - 1, 0)
    band_of = target_block // block_count
    member = ((band_of[:, None] == jnp.arange(band_count)[None, :]) & alive[:, None]).astype(
        jnp.int32
    )
    ranking = jnp.sum(jnp.cumsum(member, axis=0) * member, axis=1) - 1
    slot_of = jnp.where(alive, band_of * capacity + ranking, band_count * capacity)
    local_plus = jnp.where(alive, target_block % block_count + 1, 0)
    slot_total = band_count * capacity
    matching = slot_of[None, :] == jnp.arange(slot_total)[:, None]
    route_matrix = matching.astype(jnp.float32)
    labels = jnp.sum(jnp.where(matching, local_plus[None, :], 0), axis=1)
    return (route_matrix, labels)


def gather_slots(route_matrix, values):
    return jnp.einsum("sb,cbk->csk", route_matrix, values, precision=lax.Precision.HIGHEST)


def spread_slots(route_matrix, values):
    return jnp.einsum("sb,csk->cbk", route_matrix, values, precision=lax.Precision.HIGHEST)


def pack(values, route_matrix, labels, band_count, capacity):
    payload = gather_slots(route_matrix, values)
    return (
        payload.reshape(2, band_count, capacity, BLOCK),
        labels.reshape(1, band_count, capacity),
    )


def settle(blocks, payload, labels):
    block_count = blocks.shape[1]
    flat_payload = payload.reshape(2, -1, BLOCK)
    flat_labels = labels.reshape(-1)
    slot_selector = (flat_labels[:, None] - 1 == jnp.arange(block_count)[None, :]).astype(
        jnp.float32
    )
    alive = (flat_labels > 0).astype(jnp.float32)[None, :, None]
    picked = gather_slots(slot_selector, blocks)
    paired = match_gain * alive * (picked - flat_payload)
    reaction = spread_slots(slot_selector, paired)
    return (paired, reaction)


def per_device(disp, targets, stiffness, stiff_class, match_dest):
    field = disp[0]
    anchor = targets[0]
    row_count = field.shape[1]
    col_count = field.shape[2]
    block_count = row_count * (col_count // BLOCK)
    band_count = lax.axis_size("grid")
    capacity = max(2, 2 * block_count // band_count)
    member = (stiff_class[0][..., None] == jnp.arange(CLASSES)).astype(jnp.float32)
    kappa = jnp.repeat(jnp.sum(member * stiffness, axis=-1), BLOCK, axis=-1)
    marker = match_dest[0].reshape(block_count) + 1
    own_matrix, own_labels = placement(marker, block_count, band_count, capacity)
    velocity = jnp.zeros_like(field)
    for repeat_index in range(STEPS):
        extended = with_halo(field, (("grid", 1),), 1)
        blocks = field.reshape(2, block_count, BLOCK)
        pulled = (field - anchor).reshape(2, block_count, BLOCK)
        payload, labels = pack(pulled, own_matrix, own_labels, band_count, capacity)
        moved_payload, moved_labels = (
            lax.all_to_all(payload, "grid", split_axis=1, concat_axis=1, tiled=True),
            lax.all_to_all(labels, "grid", split_axis=1, concat_axis=1, tiled=True),
        )
        held_payload, held_labels = passed_along((moved_payload, moved_labels), "stack", 1)
        paired, reaction = settle(blocks, held_payload, held_labels)
        returned = passed_along(paired.reshape(2, band_count, capacity, BLOCK), "stack", -1)
        arrived = lax.all_to_all(returned, "grid", split_axis=1, concat_axis=1, tiled=True)
        gained = spread_slots(own_matrix, arrived.reshape(2, -1, BLOCK))
        match_force = (gained - reaction).reshape(2, row_count, col_count)
        velocity = damping * velocity + kappa * laplace(extended) + match_force
        field = field + velocity
    return (field[None], velocity[None])


TILE = 8
BAND = 256
VMEM_BYTES = 58 * 1024 * 1024


def two_pieces(value):
    high = value.astype(jnp.bfloat16)
    low = (value - high.astype(jnp.float32)).astype(jnp.bfloat16)
    return jnp.concatenate([high, low], axis=1)


def joined(pieces):
    return pieces[:, :BLOCK] + pieces[:, BLOCK:]


def relax_kernel(
    bands,
    own_ref,
    out_ref,
    data_ref,
    kappa_ref,
    out_of_inner_ref,
    in_of_outer_ref,
    in_of_far_ref,
    field_ref,
    velocity_ref,
    weight_ref,
    force_ref,
    pieces_ref,
    far_pieces_ref,
    far_ref,
    spread_ref,
    match_ref,
    swap_send,
    swap_recv,
    out_send,
    out_recv,
    out_local,
    local_sem,
    send_sem,
    recv_sem,
):
    total = bands * BAND
    tiles = BAND // TILE
    slab = lax.axis_index("slab")
    half, comp, stack = (lax.axis_index(name) for name in ("half", "comp", "stack"))
    z = half * 2 + comp
    other_z = half * 2 + 1 - comp
    x, core = stack // 2, stack % 2
    sections = (3 * core, 1 + core)
    far = 2 - core
    edge_source = 2 * core
    sibling = (slab, half, comp, x * 2 + 1 - core)
    beside = (slab, half, 1 - comp, x * 2 + core)
    across = (slab, half, 1 - comp, x * 2 + 1 - core)
    barrier = pltpu.get_barrier_semaphore()
    over_x = (slab, half, comp, (1 - x) * 2 + core)
    along = [other_z, 2 - half, 3 - 3 * half]

    def column(to_z):
        return (slab, to_z // 2, to_z % 2, stack)

    for peer in [column(to_z) for to_z in along] + [sibling, across, over_x]:
        pl.semaphore_signal(barrier, inc=1, device_id=peer, device_id_type=pl.DeviceIdType.MESH)
    pl.semaphore_wait(barrier, 6)

    started = []

    def send(source, slot, peer):
        copy = pltpu.make_async_remote_copy(
            src_ref=source,
            dst_ref=data_ref.at[slot],
            send_sem=send_sem.at[len(started)],
            recv_sem=recv_sem.at[slot],
            device_id=peer,
            device_id_type=pl.DeviceIdType.MESH,
        )
        copy.start()
        started.append(copy)

    def arrive(slot):
        pltpu.make_async_remote_copy(
            src_ref=data_ref.at[slot],
            dst_ref=data_ref.at[slot],
            send_sem=send_sem.at[0],
            recv_sem=recv_sem.at[slot],
            device_id=sibling,
            device_id_type=pl.DeviceIdType.MESH,
        ).wait_recv()

    kept = []
    for kind in range(2):
        for to_z in along:
            send(own_ref.at[to_z % 2, kind], (x, core, z, kind), column(to_z))
        send(own_ref.at[comp, kind], (x, core, z, kind), over_x)
        copy = pltpu.make_async_copy(
            own_ref.at[comp, kind], data_ref.at[x, core, z, kind], local_sem.at[kind]
        )
        copy.start()
        kept.append(copy)
    for copy in kept:
        copy.wait()

    def forward_column(kind):
        for band in along:
            slot = (x, core, band, kind)
            arrive(slot)
            send(data_ref.at[slot], slot, over_x)

    def forward_sibling(kind):
        for band in [z] + along:
            arrive((1 - x, core, band, kind))
        for band in [z] + along:
            slot = (1 - core, core, band, kind)
            send(data_ref.at[slot], slot, sibling)

    def from_sibling(kind):
        for band in [z] + along:
            arrive((core, 1 - core, band, kind))

    forward_column(0)
    forward_sibling(0)
    forward_column(1)
    from_sibling(0)

    lane = lax.broadcasted_iota(jnp.int32, (TILE, BLOCK), 1)
    sub = lax.broadcasted_iota(jnp.int32, (TILE, BLOCK), 0)

    def loaded(s, band, kind):
        return data_ref[s // 2, s % 2, band, kind, 0:BAND]

    def constant_row(s, which, band, part):
        line = BAND + 2 * which + part
        return data_ref[s // 2, s % 2, band, 0, line : line + 1]

    def as_column(row):
        return jnp.broadcast_to(row, (BLOCK, BLOCK)).T

    def rows_of(band):
        if isinstance(band, int):
            return slice(band * BAND, (band + 1) * BAND)
        return pl.ds(pl.multiple_of(band * BAND, BAND), BAND)

    def spread_band(slot, s, band):
        for k in range(tiles):
            centre = field_ref[s, band, k + 1]
            before = field_ref[s, band, k]
            after = field_ref[s, band, k + 2]
            left = pltpu.roll(jnp.where(lane == BLOCK - 1, before, centre), 1, 1)
            right = pltpu.roll(jnp.where(lane == 0, after, centre), BLOCK - 1, 1)
            spread_ref[slot, s, band + 1, k] = centre + 0.5 * (left + right)

    wide = lax.broadcasted_iota(jnp.int32, (BLOCK, BLOCK), 1).astype(jnp.float32)
    tall = lax.broadcasted_iota(jnp.int32, (BLOCK, BLOCK), 0).astype(jnp.float32)
    first = core == 0

    def build(band, carry):
        for part in range(2):
            base = band * BAND + part * BLOCK
            rows = pl.ds(pl.multiple_of(base, BLOCK), BLOCK)
            here = tall + base.astype(jnp.float32)
            for s in range(2):
                kappa_ref[s, rows] = as_column(constant_row(sections[s], 0, band, part))
            edge_column = as_column(constant_row(edge_source, 1, band, part))
            middle_column = as_column(constant_row(1, 1, band, part))
            for j in range(total // BLOCK):
                cols = slice(j * BLOCK, (j + 1) * BLOCK)
                there = wide + float(j * BLOCK)
                edge_row = constant_row(edge_source, 1, j // 2, j % 2)
                middle_row = constant_row(1, 1, j // 2, j % 2)
                pick = jnp.where(edge_column == there, 1.0, 0.0)
                drop = jnp.where(edge_row == here, 1.0, 0.0)
                out_of_inner_ref[rows, cols] = jnp.where(first, pick, drop).astype(jnp.bfloat16)
                in_of_outer_ref[rows, cols] = jnp.where(first, drop, pick).astype(jnp.bfloat16)
                pick = jnp.where(middle_column == there, 1.0, 0.0)
                drop = jnp.where(middle_row == here, 1.0, 0.0)
                in_of_far_ref[rows, cols] = jnp.where(first, pick, drop).astype(jnp.bfloat16)
        return carry

    lax.fori_loop(0, bands, build, 0)

    edge = jnp.zeros((tiles, TILE, BLOCK), jnp.float32)
    for s in range(2):
        for slot in range(2):
            spread_ref[slot, s, 0] = edge
            spread_ref[slot, s, bands + 1] = edge

    def begin(band, carry):
        rows = rows_of(band)
        for s in range(2):
            field_ref[s, band, 0] = edge[0]
            field_ref[s, band, tiles + 1] = edge[0]
            value = loaded(sections[s], band, 0)
            field_ref[s, band, 1 : tiles + 1] = value.reshape(tiles, TILE, BLOCK)
            pieces_ref[0, s, rows] = two_pieces(value)
            velocity_ref[s, band] = edge
            spread_band(0, s, band)
        return carry

    lax.fori_loop(0, bands, begin, 0)

    forward_sibling(1)
    from_sibling(1)

    def offsets(band, carry):
        rows = rows_of(band)
        for s in range(2):
            pieces_ref[1, s, rows] = two_pieces(loaded(sections[s], band, 1))
        far_pieces_ref[rows] = two_pieces(loaded(far, band, 1))
        return carry

    lax.fori_loop(0, bands, offsets, 0)

    ones = jnp.ones((total, BLOCK), jnp.bfloat16)

    def product(matrix, values):
        return jnp.dot(matrix, values, preferred_element_type=jnp.float32)

    def constants(band, carry):
        rows = rows_of(band)
        out_rows, in_rows, far_rows = (
            out_of_inner_ref[rows],
            in_of_outer_ref[rows],
            in_of_far_ref[rows],
        )
        count_out, count_in, count_far = (
            product(matrix, ones) for matrix in (out_rows, in_rows, far_rows)
        )
        weight_ref[0, rows] = 8.0 * kappa_ref[0, rows] + match_gain * count_out
        weight_ref[1, rows] = 8.0 * kappa_ref[1, rows] + match_gain * (count_in + count_far)
        ahead = count_out * loaded(sections[0], band, 1)
        behind = joined(product(out_rows, pieces_ref[1, 1]))
        force_ref[0, rows] = match_gain * jnp.where(first, ahead, -behind)
        alive = jnp.where(first, count_far, count_in)
        from_outer = joined(product(in_rows, pieces_ref[1, 0]))
        from_far = joined(product(far_rows, far_pieces_ref[...]))
        behind = jnp.where(first, from_outer, from_far)
        force_ref[1, rows] = match_gain * (alive * loaded(sections[1], band, 1) - behind)
        return carry

    lax.fori_loop(0, bands, constants, 0)

    def far_start(band, carry):
        far_pieces_ref[rows_of(band)] = two_pieces(loaded(far, band, 0))
        return carry

    lax.fori_loop(0, bands, far_start, 0)

    def swap(slot, band):
        return pltpu.make_async_remote_copy(
            src_ref=field_ref.at[1, band, pl.ds(1, tiles)],
            dst_ref=far_ref.at[slot, band],
            send_sem=swap_send.at[band],
            recv_sem=swap_recv.at[slot, band],
            device_id=sibling,
            device_id_type=pl.DeviceIdType.MESH,
        )

    def match_band(s, band, now, buffer):
        rows = rows_of(band)
        if s == 0:
            sums = product(out_of_inner_ref[rows], pieces_ref[now, 1])
        else:
            sums = product(in_of_outer_ref[rows], pieces_ref[now, 0])
            sums = sums + product(in_of_far_ref[rows], far_pieces_ref[...])
        match_ref[buffer] = joined(sums)

    def move_band(s, band, now, later, buffer):
        base = band * BAND if isinstance(band, int) else pl.multiple_of(band * BAND, BAND)
        for k in range(0, tiles, 2):
            pair = []
            for q in (k, k + 1):
                spot = pl.ds(base + q * TILE, TILE)
                here = spread_ref[now, s, band + 1, q]
                above = spread_ref[now, s, band, q]
                below = spread_ref[now, s, band + 2, q]
                up = pltpu.roll(jnp.where(sub == TILE - 1, above, here), 1, 0)
                down = pltpu.roll(jnp.where(sub == 0, below, here), TILE - 1, 0)
                field = field_ref[s, band, q + 1]
                velocity = (
                    damping * velocity_ref[s, band, q]
                    + kappa_ref[s, spot] * (2.0 * here + up + down)
                    - weight_ref[s, spot] * field
                    + match_gain * match_ref[buffer, q * TILE : (q + 1) * TILE]
                    + force_ref[s, spot]
                )
                field = field + velocity
                velocity_ref[s, band, q] = velocity
                field_ref[s, band, q + 1] = field
                pair.append(field)
            spot = pl.ds(base + k * TILE, 2 * TILE)
            pieces_ref[later, s, spot] = two_pieces(jnp.concatenate(pair, axis=0))

    def one_band(s, band, now, later):
        match_band(s, band, now, 0)
        move_band(s, band, now, later, 0)

    tasks = [(s, band) for s in (1, 0) for band in range(bands)]

    def step(now):
        later = 1 - now
        match_band(*tasks[0], now, 0)
        for turn, (s, band) in enumerate(tasks):
            if turn + 1 < len(tasks):
                match_band(*tasks[turn + 1], now, (turn + 1) % 2)
            move_band(s, band, now, later, turn % 2)
            if s == 1:
                swap(now, band).start()
            spread_band(later, s, band)

        def arrived(band, inside):
            swap(now, band).wait()
            value = far_ref[now, band].reshape(BAND, BLOCK)
            far_pieces_ref[rows_of(band)] = two_pieces(value)
            return inside

        lax.fori_loop(0, bands, arrived, 0)

    def two_steps(t, carry):
        step(0)
        step(1)
        return carry

    lax.fori_loop(0, (STEPS - 1) // 2, two_steps, 0)
    if STEPS % 2 == 0:
        step(0)

    now = (STEPS - 1) % 2
    sends = core == x

    def parts_of(s, band):
        return (field_ref.at[s, band, pl.ds(1, tiles)], velocity_ref.at[s, band])

    def deliver(s, band, peer, count):
        return [
            pltpu.make_async_remote_copy(
                src_ref=source,
                dst_ref=out_ref.at[comp, kind],
                send_sem=out_send.at[count, kind],
                recv_sem=out_recv.at[comp, kind],
                device_id=peer,
                device_id_type=pl.DeviceIdType.MESH,
            )
            for kind, source in enumerate(parts_of(s, band))
        ]

    def keep():
        return [
            pltpu.make_async_copy(source, out_ref.at[comp, kind], out_local.at[kind])
            for kind, source in enumerate(parts_of(0, z))
        ]

    def landed(which):
        return [
            pltpu.make_async_remote_copy(
                src_ref=out_ref.at[which, kind],
                dst_ref=out_ref.at[which, kind],
                send_sem=out_send.at[0, kind],
                recv_sem=out_recv.at[which, kind],
                device_id=sibling,
                device_id_type=pl.DeviceIdType.MESH,
            )
            for kind in range(2)
        ]

    @pl.when(sends)
    def _():
        one_band(1, other_z, now, 1 - now)
        for copy in deliver(1, other_z, across, 0):
            copy.start()
        one_band(0, other_z, now, 1 - now)
        for copy in deliver(0, other_z, beside, 1):
            copy.start()
        one_band(1, z, now, 1 - now)
        for copy in deliver(1, z, sibling, 2):
            copy.start()
        one_band(0, z, now, 1 - now)
        for copy in keep():
            copy.start()
        for copy in deliver(1, other_z, across, 0):
            copy.wait_send()
        for copy in deliver(0, other_z, beside, 1):
            copy.wait_send()
        for copy in deliver(1, z, sibling, 2):
            copy.wait_send()
        for copy in keep():
            copy.wait()

    @pl.when(jnp.logical_not(sends))
    def _():
        for copy in landed(comp):
            copy.wait_recv()

    for copy in landed(1 - comp):
        copy.wait_recv()
    for copy in started:
        copy.wait_send()


def tiled_order(value):
    lead = value.shape[:-2]
    rows, cols = value.shape[-2:]
    split = value.reshape(*lead, rows, cols // BLOCK, BLOCK)
    return jnp.swapaxes(split, -3, -2).reshape(*lead, rows * (cols // BLOCK), BLOCK)


def whole_component(disp, targets, stiffness, stiff_class, match_dest):
    sections = lax.axis_size("stack")
    bands = lax.axis_size("half") * 2
    blocks_row = stiff_class.shape[-1]
    total = bands * BAND
    tiles = BAND // TILE
    member = (stiff_class[0][..., None] == jnp.arange(CLASSES)).astype(jnp.float32)
    kappa = jnp.sum(member * stiffness, axis=-1)
    dest = match_dest[0]
    row, col = dest // blocks_row, dest % blocks_row
    dest = jnp.where(dest >= 0, (row // TILE) * BAND + col * TILE + row % TILE, -1)
    constants = jnp.stack([kappa.T, dest.astype(jnp.float32).T]).reshape(4, BLOCK)
    constants = jnp.pad(constants, ((0, TILE - 4), (0, 0)))
    both = tiled_order(jnp.stack([disp[0], targets[0]], axis=1))
    extra = jnp.broadcast_to(constants, (2, 2, TILE, BLOCK))
    both = jnp.concatenate([both, extra], axis=2)
    result = pl.pallas_call(
        functools.partial(relax_kernel, bands),
        out_shape=jax.ShapeDtypeStruct((2, 2, tiles, TILE, BLOCK), jnp.float32),
        in_specs=[pl.BlockSpec(memory_space=pltpu.VMEM)],
        out_specs=pl.BlockSpec(memory_space=pltpu.VMEM),
        scratch_shapes=[
            pltpu.VMEM((sections // 2, 2, bands, 2, BAND + TILE, BLOCK), jnp.float32),
            pltpu.VMEM((2, total, BLOCK), jnp.float32),
            pltpu.VMEM((total, total), jnp.bfloat16),
            pltpu.VMEM((total, total), jnp.bfloat16),
            pltpu.VMEM((total, total), jnp.bfloat16),
            pltpu.VMEM((2, bands, tiles + 2, TILE, BLOCK), jnp.float32),
            pltpu.VMEM((2, bands, tiles, TILE, BLOCK), jnp.float32),
            pltpu.VMEM((2, total, BLOCK), jnp.float32),
            pltpu.VMEM((2, total, BLOCK), jnp.float32),
            pltpu.VMEM((2, 2, total, 2 * BLOCK), jnp.bfloat16),
            pltpu.VMEM((total, 2 * BLOCK), jnp.bfloat16),
            pltpu.VMEM((2, bands, tiles, TILE, BLOCK), jnp.float32),
            pltpu.VMEM((2, 2, bands + 2, tiles, TILE, BLOCK), jnp.float32),
            pltpu.VMEM((2, BAND, BLOCK), jnp.float32),
            pltpu.SemaphoreType.DMA((bands,)),
            pltpu.SemaphoreType.DMA((2, bands)),
            pltpu.SemaphoreType.DMA((3, 2)),
            pltpu.SemaphoreType.DMA((2, 2)),
            pltpu.SemaphoreType.DMA((2,)),
            pltpu.SemaphoreType.DMA((2,)),
            pltpu.SemaphoreType.DMA((22,)),
            pltpu.SemaphoreType.DMA((sections // 2, 2, bands, 2)),
        ],
        compiler_params=pltpu.CompilerParams(
            collective_id=0, has_side_effects=True, vmem_limit_bytes=VMEM_BYTES
        ),
    )(both)
    result = result.reshape(2, 2, tiles, TILE, BLOCK).transpose(1, 0, 3, 2, 4)
    result = result.reshape(2, 1, 2, TILE, tiles * BLOCK)
    return (result[0], result[1])


def solution(mesh):
    by_name = mesh.shape
    if by_name["grid"] == 4 and by_name["stack"] == 4:
        inner = Mesh(
            mesh.devices.reshape(by_name["slab"], by_name["grid"] // 2, 2, by_name["stack"]),
            ("slab", "half", "comp", "stack"),
        )
        body, grid = whole_component, ("half", "comp")
    else:
        inner, body, grid = mesh, per_device, "grid"
    return jax.shard_map(
        body,
        mesh=inner,
        in_specs=(
            P(("slab", "stack"), None, grid, None),
            P(("slab", "stack"), None, grid, None),
            P(),
            P(("slab", "stack"), grid, None),
            P(("slab", "stack"), grid, None),
        ),
        out_specs=(
            P(("slab", "stack"), None, grid, None),
            P(("slab", "stack"), None, grid, None),
        ),
        check_vma=False,
    )
```
